32 devices in a mesh: seed: 4 (over y, x), tok: 8 (over z, core).
Axes of the slice: x: 2, y: 2, z: 4, core: 2. Of those that a mesh axis runs over, the one named last changes fastest.
Arguments:
- atom_feats: bfloat16 [8192, 8, 128], P('tok', 'seed'), may hold values from -6 to 6
- atom_index: int32 [8192], P('tok'), may hold values from 0 to 1023, as said below
- token_cond: bfloat16 [1024, 768], P('tok'), may hold values from -6 to 6
- pair_bias: bfloat16 [16, 1024, 1024], P('seed', 'tok'), may hold values from -8 to 248
- atom_bias_enc: bfloat16 [8192, 4, 128], P('tok'), may hold values from -8 to 248
- atom_bias_dec: bfloat16 [8192, 4, 128], P('tok'), may hold values from -8 to 248
- enc_project: bfloat16 [128, 384], replicated, may hold values from -0.5 to 0.5
- enc_mix: bfloat16 [128, 128], replicated, may hold values from -0.5 to 0.5
- pool_weight: bfloat16 [128, 768], replicated, may hold values from -0.5 to 0.5
- token_project: bfloat16 [768, 3072], replicated, may hold values from -0.21875 to 0.21875
- token_mix: bfloat16 [768, 768], replicated, may hold values from -0.21875 to 0.21875
- swiglu_in: bfloat16 [768, 3072], replicated, may hold values from -0.21875 to 0.21875
- swiglu_out: bfloat16 [1536, 768], replicated, may hold values from -0.15625 to 0.15625
- spread_weight: bfloat16 [768, 128], replicated, may hold values from -0.21875 to 0.21875
- dec_project: bfloat16 [128, 384], replicated, may hold values from -0.5 to 0.5
- dec_mix: bfloat16 [128, 128], replicated, may hold values from -0.5 to 0.5
Outputs:
- token_state: bfloat16 [1024, 8, 768], P('tok', 'seed')
- atom_update: bfloat16 [8192, 8, 128], P('tok', 'seed')
The draws below stay inside these ranges and needn't reach their ends.
Inputs may be any that keep to these rules, and one draw needn't show every extreme that they name: `atom_index`: Nondecreasing. The atoms of token t are rows 8 t + e(t) to 8 (t + 1) + e(t + 1) - 1, every e between -3 and 3, e(0) = e(1024) = 0, and e(t) between -3 and -2 for every other t that is a multiple of 128; so every token has 2 to 14 atoms.
All inputs are finite; a program needn't handle non-finite values.
Results may differ from the reference program's by a relative error of at most 0.015.
Values may be sent and summed in bfloat16 or wider, within the bound.
A program may use at most 192 MiB of HBM per device.

```python
import jax
import jax.numpy as jnp
from jax import lax

CT = 768
HEADS = 16
CA = 128
ATOM_HEADS = 4
QUERY_BLOCK = 32
KEY_WINDOW = 128
ATOMS_PER_TOKEN = 8
TOK_DEV = 128
HEAD_SIZE = 48
ATOM_HEAD_SIZE = 32
TRANS = 1536
TOKENS = 1024
ATOMS = 8192
SEEDS = 8


def clipped_normal(key, shape):
    return jnp.clip(jax.random.normal(jax.random.fold_in(key, 1), shape, jnp.float32), -4.0, 4.0)


def draw_atom_index(key, part):
    key = jax.random.fold_in(key, 5)
    bounds = jnp.arange(TOKENS + 1, dtype=jnp.int32)
    offsets = jax.random.randint(key, (TOKENS + 1,), -3, 4)
    edge_offsets = jax.random.randint(jax.random.fold_in(key, 9), (TOKENS + 1,), -3, -1)
    offsets = jnp.where(bounds % TOK_DEV == 0, edge_offsets, offsets)
    offsets = jnp.where((bounds == 0) | (bounds == TOKENS), 0, offsets)
    starts = ATOMS_PER_TOKEN * bounds + offsets
    atoms = jnp.arange(ATOMS, dtype=jnp.int32)
    guess = atoms // ATOMS_PER_TOKEN
    here = jnp.take(starts, guess)
    after = jnp.take(starts, jnp.minimum(guess + 1, TOKENS))
    found = guess - 1 + (here <= atoms).astype(jnp.int32) + (after <= atoms).astype(jnp.int32)
    return found.astype(jnp.int32)


def draw_pair_bias(key, part):
    key = jax.random.fold_in(key, 11)
    shape = (HEADS, TOKENS, TOKENS)
    base = clipped_normal(key, shape)
    return base.astype(jnp.bfloat16)


def draw_atom_bias_enc(key, part):
    key = jax.random.fold_in(key, 12)
    shape = (ATOMS, ATOM_HEADS, KEY_WINDOW)
    base = clipped_normal(key, shape)
    return base.astype(jnp.bfloat16)


def draw_atom_bias_dec(key, part):
    key = jax.random.fold_in(key, 13)
    shape = (ATOMS, ATOM_HEADS, KEY_WINDOW)
    base = clipped_normal(key, shape)
    return base.astype(jnp.bfloat16)


def steps_of(stream_key, dims, split, low, largest):
    level = 1.0
    for dim, shards_of in split:
        steps = jax.random.uniform(jax.random.fold_in(jax.random.fold_in(stream_key, 6), dim), (shards_of,), jnp.float32, low / len(split), largest / len(split))
        level = level * jnp.repeat(jnp.exp(steps), dims[dim] // shards_of).reshape((-1,) + (1,) * (len(dims) - 1 - dim))
    return level


def gaussian(own_key, shape, scale, bound, shards=(), kind=jnp.bfloat16):
    loudness = steps_of(own_key, shape, shards, -0.22, 0.18) if shards else 1.0
    values = jax.random.normal(own_key, shape, jnp.float32) * scale * loudness
    return jnp.minimum(jnp.maximum(values, -bound), bound).astype(kind)


def setup_inputs(seed: int = 0) -> dict:
    seeds = jax.random.split(jax.random.key(seed), 17)
    atom_feats = gaussian(seeds[0], (ATOMS, SEEDS, CA), 1.0, 6.0, ((0, 8), (1, 4)))
    atom_index = draw_atom_index(jax.random.fold_in(seeds[16], 71), 0)
    token_cond = gaussian(seeds[2], (TOKENS, CT), 1.0, 6.0, ((0, 8),))
    pair_bias = draw_pair_bias(jax.random.fold_in(seeds[16], 71), 0)
    atom_bias_enc = draw_atom_bias_enc(jax.random.fold_in(seeds[16], 71), 0)
    atom_bias_dec = draw_atom_bias_dec(jax.random.fold_in(seeds[16], 71), 0)
    enc_project = gaussian(seeds[6], (CA, 3 * CA), CA ** -0.5, 0.5)
    enc_mix = gaussian(seeds[7], (CA, CA), CA ** -0.5, 0.5)
    pool_weight = gaussian(seeds[8], (CA, CT), CA ** -0.5, 0.5)
    token_project = gaussian(seeds[9], (CT, 4 * CT), CT ** -0.5, 0.21875)
    token_mix = gaussian(seeds[10], (CT, CT), CT ** -0.5, 0.21875)
    swiglu_in = gaussian(seeds[11], (CT, 2 * TRANS), CT ** -0.5, 0.21875)
    swiglu_out = gaussian(seeds[12], (TRANS, CT), TRANS ** -0.5, 0.15625)
    spread_weight = gaussian(seeds[13], (CT, CA), CT ** -0.5, 0.21875)
    dec_project = gaussian(seeds[14], (CA, 3 * CA), CA ** -0.5, 0.5)
    dec_mix = gaussian(seeds[15], (CA, CA), CA ** -0.5, 0.5)
    return {"atom_feats": atom_feats, "atom_index": atom_index, "token_cond": token_cond, "pair_bias": pair_bias, "atom_bias_enc": atom_bias_enc, "atom_bias_dec": atom_bias_dec, "enc_project": enc_project, "enc_mix": enc_mix, "pool_weight": pool_weight, "token_project": token_project, "token_mix": token_mix, "swiglu_in": swiglu_in, "swiglu_out": swiglu_out, "spread_weight": spread_weight, "dec_project": dec_project, "dec_mix": dec_mix}


EPS = 1e-05
NEGATIVE = -1000000000.0

def layer_norm(values):
    centre = values - lax.optimization_barrier(jnp.mean(values, axis=-1, keepdims=True))
    variance = lax.optimization_barrier(jnp.mean(centre * centre, axis=-1, keepdims=True))
    return centre * lax.rsqrt(variance + EPS)

def window_attend(packed, bias):
    atom_total = packed.shape[0]
    block_count = atom_total // QUERY_BLOCK
    margin = (KEY_WINDOW - QUERY_BLOCK) // 2
    extra_tiles = KEY_WINDOW // QUERY_BLOCK - 1
    queries = packed[:, :CA].astype(jnp.float32).reshape(block_count, QUERY_BLOCK, ATOM_HEADS, ATOM_HEAD_SIZE)
    padded = jnp.pad(packed[:, CA:], ((margin, margin), (0, 0)))
    key_tiles = padded.reshape(block_count + extra_tiles, QUERY_BLOCK, 2 * CA)
    windows = jnp.concatenate([key_tiles[offset:offset + block_count] for offset in range(extra_tiles + 1)], axis=1)
    key_rows = windows[:, :, :CA].astype(jnp.float32).reshape(block_count, KEY_WINDOW, ATOM_HEADS, ATOM_HEAD_SIZE)
    value_rows = windows[:, :, CA:].astype(jnp.float32).reshape(block_count, KEY_WINDOW, ATOM_HEADS, ATOM_HEAD_SIZE)
    scores = jnp.einsum('bqhd,bkhd->bhqk', queries, key_rows) * ATOM_HEAD_SIZE ** (-0.5)
    scores = scores + bias.astype(jnp.float32).reshape(block_count, QUERY_BLOCK, ATOM_HEADS, KEY_WINDOW).transpose(0, 2, 1, 3)
    position = QUERY_BLOCK * jnp.arange(block_count, dtype=jnp.int32)[:, None] - margin + jnp.arange(KEY_WINDOW, dtype=jnp.int32)[None, :]
    in_range = (position >= 0) & (position < atom_total)
    scores = jnp.where(in_range[:, None, None, :], scores, NEGATIVE)
    row_max = lax.optimization_barrier(jnp.max(scores, axis=-1, keepdims=True))
    weights = jnp.exp(scores - row_max)
    rounded = lax.optimization_barrier(weights.astype(jnp.bfloat16)).astype(jnp.float32)
    attended_atoms = jnp.einsum('bhqk,bkhd->bqhd', rounded, value_rows)
    attended_atoms = attended_atoms / lax.optimization_barrier(jnp.sum(weights, axis=-1)).transpose(0, 2, 1)[..., None]
    return attended_atoms.reshape(atom_total, CA).astype(jnp.bfloat16)

def atom_block(inputs, bias, project, mix):
    normed = layer_norm(inputs.astype(jnp.float32)).astype(jnp.bfloat16)
    packed = jnp.dot(normed, project, preferred_element_type=jnp.float32).astype(jnp.bfloat16)
    attended_atoms = window_attend(packed, bias)
    return (inputs.astype(jnp.float32) + jnp.dot(attended_atoms, mix, preferred_element_type=jnp.float32)).astype(jnp.bfloat16)

def head_attend(operands):
    head_query, head_key, head_value, head_bias = operands
    scores = jnp.dot(head_query, head_key.T, preferred_element_type=jnp.float32) * HEAD_SIZE ** (-0.5)
    scores = scores + head_bias.astype(jnp.float32)
    row_max = lax.optimization_barrier(jnp.max(scores, axis=-1, keepdims=True))
    weights = jnp.exp(scores - row_max)
    rounded = lax.optimization_barrier(weights.astype(jnp.bfloat16))
    summed = jnp.dot(rounded, head_value, preferred_element_type=jnp.float32)
    return summed / lax.optimization_barrier(jnp.sum(weights, axis=-1, keepdims=True))

def split_heads(values):
    return values.reshape(TOKENS, HEADS, HEAD_SIZE).transpose(1, 0, 2)

def reference(atom_feats, atom_index, token_cond, pair_bias, atom_bias_enc, atom_bias_dec, enc_project, enc_mix, pool_weight, token_project, token_mix, swiglu_in, swiglu_out, spread_weight, dec_project, dec_mix):
    counts = jax.ops.segment_sum(jnp.ones(atom_index.shape, jnp.float32), atom_index, num_segments=TOKENS)

    def one_seed(atoms):
        encoded = atom_block(atoms, atom_bias_enc, enc_project, enc_mix)
        lifted = jnp.maximum(jnp.dot(encoded, pool_weight, preferred_element_type=jnp.float32), 0.0).astype(jnp.bfloat16)
        pooled_sum = jax.ops.segment_sum(lifted.astype(jnp.float32), atom_index, num_segments=TOKENS)
        residual = token_cond.astype(jnp.float32) + pooled_sum / counts[:, None]
        normed = layer_norm(residual).astype(jnp.bfloat16)
        projected = jnp.dot(normed, token_project, preferred_element_type=jnp.float32)
        queries = projected[:, :CT].astype(jnp.bfloat16)
        key_rows = projected[:, CT:2 * CT].astype(jnp.bfloat16)
        value_rows = projected[:, 2 * CT:3 * CT].astype(jnp.bfloat16)
        gate_open = jax.nn.sigmoid(projected[:, 3 * CT:])
        attended = lax.map(head_attend, (split_heads(queries), split_heads(key_rows), split_heads(value_rows), pair_bias))
        attended = attended.transpose(1, 0, 2).reshape(TOKENS, CT)
        gated_out = (attended * gate_open).astype(jnp.bfloat16)
        residual = residual + jnp.dot(gated_out, token_mix, preferred_element_type=jnp.float32)
        widened = jnp.dot(layer_norm(residual).astype(jnp.bfloat16), swiglu_in, preferred_element_type=jnp.float32)
        hidden = (jax.nn.silu(widened[:, :TRANS]) * widened[:, TRANS:]).astype(jnp.bfloat16)
        token_state = (residual + jnp.dot(hidden, swiglu_out, preferred_element_type=jnp.float32)).astype(jnp.bfloat16)
        spread = jnp.dot(token_state, spread_weight, preferred_element_type=jnp.float32).astype(jnp.bfloat16)
        decoded_in = (encoded.astype(jnp.float32) + spread[atom_index].astype(jnp.float32)).astype(jnp.bfloat16)
        atom_update = atom_block(decoded_in, atom_bias_dec, dec_project, dec_mix)
        return (token_state, atom_update)
    token_state, atom_update = lax.map(one_seed, atom_feats.transpose(1, 0, 2))
    return (token_state.transpose(1, 0, 2), atom_update.transpose(1, 0, 2))
```

```python
import functools

import jax
import jax.numpy as jnp
from jax import lax
from jax.experimental import pallas as pl
from jax.experimental.pallas import tpu as pltpu
from jax.sharding import PartitionSpec as P

HEADS = 16
QUERY_BLOCK = 32
EPS = 1e-05
NEGATIVE = -1000000000.0
HALO = 128
RIM = 64
EDGE = 8
MISSING = -1000
BF = jnp.bfloat16
F32 = jnp.float32


def layer_norm(values):
    centre = values - jnp.mean(values, axis=-1, keepdims=True)
    variance = jnp.mean(centre * centre, axis=-1, keepdims=True)
    return centre * lax.rsqrt(variance + EPS)


def mm(a, b):
    return jnp.dot(a, b, preferred_element_type=F32)


def mm_t(a, b):
    return lax.dot_general(a, b, (((1,), (1,)), ((), ())), preferred_element_type=F32)


def iota(shape, dim):
    return lax.broadcasted_iota(jnp.int32, shape, dim)


def window_attention(packed, bias, mixed, blocks, key_base, low, high, group):
    seeds, _, triple = packed.shape
    width = triple // 3
    window = bias.shape[1]
    heads = bias.shape[0] // mixed.shape[1]
    size = width // heads
    rows = QUERY_BLOCK * heads
    margin = (window - QUERY_BLOCK) // 2
    repeat = (iota((rows, QUERY_BLOCK), 0) // heads == iota((rows, QUERY_BLOCK), 1)).astype(BF)
    join = (iota((QUERY_BLOCK, rows), 1) // heads == iota((QUERY_BLOCK, rows), 0)).astype(BF)
    own = (iota((rows, width), 0) % heads) == (iota((rows, width), 1) // size)
    lane = iota((rows, window), 1)

    def step(i, carry):
        for g in range(group):
            j = i * group + g
            start = pl.multiple_of(key_base + QUERY_BLOCK * j, 16)
            first = pl.multiple_of(QUERY_BLOCK * j, QUERY_BLOCK)
            term = bias[pl.ds(pl.multiple_of(rows * j, rows), rows), :].astype(F32)
            spot = lane + start
            valid = (spot >= low) & (spot < high)
            for s in range(seeds):
                query = packed[s, pl.ds(pl.multiple_of(start + margin, 16), QUERY_BLOCK), :width]
                query = jnp.where(own, mm(repeat, query), 0.0).astype(BF)
                keys = packed[s, pl.ds(start, window), width : 2 * width]
                values = packed[s, pl.ds(start, window), 2 * width :]
                scores = mm_t(query, keys) * size ** (-0.5) + term
                scores = jnp.where(valid, scores, NEGATIVE)
                weights = jnp.exp(scores - jnp.max(scores, axis=-1, keepdims=True))
                total = jnp.sum(weights, axis=-1, keepdims=True)
                part = mm(weights.astype(BF), values) / total
                part = jnp.where(own, part, 0.0).astype(BF)
                mixed[s, pl.ds(first, QUERY_BLOCK), :] = mm(join, part).astype(BF)
        return carry

    lax.fori_loop(0, blocks // group, step, 0)


def limits(tok, count, front, inner, total):
    low = jnp.where(tok == 0, front, 0)
    high = jnp.where(tok == count - 1, front + inner, total)
    return low, high


def encode_kernel(count, x, bias, index, cond, project, mix, pool, enc, residual, normed, packed, mixed):
    seeds, total, width = x.shape
    rows = mixed.shape[1]
    inner = rows - 2 * RIM
    low, high = limits(lax.axis_index("tok"), count, HALO, inner, total)
    for s in range(seeds):
        for at in range(0, total, 256):
            part = layer_norm(x[s, at : at + 256, :].astype(F32)).astype(BF)
            packed[s, at : at + 256, :] = mm(part, project[...]).astype(BF)
    window_attention(packed, bias, mixed, rows // QUERY_BLOCK, HALO - RIM - 48, low, high, 4)
    tokens = cond.shape[0]
    chosen = index[...] == iota((tokens, rows), 0)
    counts = jnp.sum(chosen.astype(F32), axis=1, keepdims=True)
    chosen = chosen.astype(BF)
    chunk = rows // 3
    for s in range(seeds):
        sums = jnp.zeros(residual.shape[1:], F32)
        for at in range(0, rows, chunk):
            base = x[s, at + HALO - RIM : at + HALO - RIM + chunk, :].astype(F32)
            part = (base + mm(mixed[s, at : at + chunk, :], mix[...])).astype(BF)
            enc[s, at : at + chunk, :] = part
            lifted = jnp.maximum(mm(part, pool[...]), 0.0).astype(BF)
            sums = sums + mm(chosen[:, at : at + chunk], lifted)
        state = cond[...].astype(F32) + sums / counts
        residual[s] = state
        normed[s] = layer_norm(state).astype(BF)


def token_kernel(
    own, everyone, bias_hbm, residual, project, mix_hbm, wide_hbm, down_hbm, spread_w,
    state_out, spread_out,
    kv, query, gate, attended, bias, mix, wide, down, sems,
):
    count, seeds, tokens, width = everyone.shape
    heads = bias.shape[0]
    size = width // heads
    copies = [
        pltpu.make_async_copy(source, target, sems.at[i])
        for i, (source, target) in enumerate(
            ((bias_hbm, bias), (mix_hbm, mix), (wide_hbm, wide), (down_hbm, down))
        )
    ]
    for copy in copies:
        copy.start()
    flat = own[...].reshape(seeds * tokens, width)
    query[...] = mm(flat, project[:, :width]).astype(BF).reshape(seeds, tokens, width)
    gate[...] = jax.nn.sigmoid(mm(flat, project[:, 3 * width :]))
    for s in range(seeds):
        for c in range(0, count, 2):
            part = everyone[c : c + 2, s].reshape(2 * tokens, width)
            for at in range(0, 2 * width, width):
                kv[s, c * tokens : (c + 2) * tokens, at : at + width] = mm(
                    part, project[:, width + at : 2 * width + at]
                ).astype(BF)
    copies[0].wait()
    span = 384
    group = span // size

    def step(i, carry):
        s = i // (heads // group)
        g = i % (heads // group)
        left = pl.multiple_of(g * span, 128)
        tiles = [jnp.zeros((tokens, 128), F32) for _ in range(span // 128)]
        for h in range(group):
            first = size * h // 128
            last = (size * h + size - 1) // 128
            wide_here = (last - first + 1) * 128
            lanes = pl.ds(left + first * 128, wide_here)
            spot = iota((tokens, wide_here), 1) + first * 128
            mine = (spot >= size * h) & (spot < size * (h + 1))
            q = query[s, :, lanes]
            q = jnp.where(mine, q, jnp.zeros_like(q))
            keys = kv[s, :, lanes]
            values = kv[s, :, pl.ds(left + width + first * 128, wide_here)]
            scores = mm_t(q, keys) * size ** (-0.5) + bias[g * group + h].astype(F32)
            weights = jnp.exp(scores - jnp.max(scores, axis=-1, keepdims=True))
            sums = jnp.sum(weights, axis=-1, keepdims=True)
            part = jnp.where(mine, mm(weights.astype(BF), values) / sums, 0.0)
            for t in range(first, last + 1):
                tiles[t] = tiles[t] + part[:, (t - first) * 128 : (t - first + 1) * 128]
        for t, tile in enumerate(tiles):
            attended[s, :, pl.ds(left + t * 128, 128)] = tile
        return carry

    lax.fori_loop(0, seeds * (heads // group), step, 0)
    copies[1].wait()
    gated = (attended[...].reshape(seeds * tokens, width) * gate[...]).astype(BF)
    state = residual[...].reshape(seeds * tokens, width) + mm(gated, mix[...])
    part = layer_norm(state).astype(BF)
    copies[2].wait()
    inner = down.shape[0]
    hidden = (jax.nn.silu(mm(part, wide[:, :inner])) * mm(part, wide[:, inner:])).astype(BF)
    copies[3].wait()
    state = (state + mm(hidden, down[...])).astype(BF)
    state_out[...] = state.reshape(seeds, tokens, width)
    spread_out[...] = mm(state, spread_w[...]).astype(BF).reshape(spread_out.shape)


def decode_kernel(count, enc, spread, index, bias, project, mix, out, decoded, packed, mixed):
    seeds, rows, width = enc.shape
    inner = out.shape[1]
    low, high = limits(lax.axis_index("tok"), count, RIM, inner, rows)
    picker = (index[...] == iota((spread.shape[1], rows), 0) - EDGE).astype(BF)
    chunk = rows // 3
    for s in range(seeds):
        for at in range(0, rows, chunk):
            carried = lax.dot_general(
                picker[:, at : at + chunk], spread[s], (((0,), (0,)), ((), ())),
                preferred_element_type=F32,
            )
            part = (enc[s, at : at + chunk, :].astype(F32) + carried).astype(BF)
            decoded[s, at : at + chunk, :] = part
            part = layer_norm(part.astype(F32)).astype(BF)
            packed[s, at : at + chunk, :] = mm(part, project[...]).astype(BF)
    window_attention(packed, bias, mixed, inner // QUERY_BLOCK, RIM - 48, low, high, 4)
    for s in range(seeds):
        for at in range(0, inner, 256):
            base = decoded[s, RIM + at : RIM + at + 256, :].astype(F32)
            out[s, at : at + 256, :] = (base + mm(mixed[s, at : at + 256, :], mix[...])).astype(BF)


PARAMS = pltpu.CompilerParams(vmem_limit_bytes=50 * 1024 * 1024)


def exchange(to_above, to_below):
    count = lax.axis_size("tok")
    above = [(i, i + 1) for i in range(count - 1)]
    below = [(target, source) for source, target in above]
    return lax.ppermute(to_above, "tok", above), lax.ppermute(to_below, "tok", below)


def per_device(
    atom_feats, atom_index, token_cond, pair_bias, atom_bias_enc, atom_bias_dec,
    enc_project, enc_mix, pool_weight, token_project, token_mix, swiglu_in, swiglu_out,
    spread_weight, dec_project, dec_mix,
):
    atoms, seeds, width = atom_feats.shape
    tokens, token_width = token_cond.shape
    atom_heads, window = atom_bias_enc.shape[1:]
    count = lax.axis_size("tok")
    tok = lax.axis_index("tok")
    whole_bias = lax.all_gather(pair_bias, "seed", axis=0, tiled=True)

    relative = atom_index - tok * tokens
    x = atom_feats.transpose(1, 0, 2)
    enc_bias = atom_bias_enc.reshape(atoms * atom_heads, window)
    dec_bias = atom_bias_dec.reshape(atoms * atom_heads, window)

    def parcel(at, at_rim):
        row = jnp.zeros((8, width), BF).at[0, :RIM].set(relative[at_rim : at_rim + RIM].astype(BF))
        rim = atom_heads * at_rim
        return jnp.concatenate(
            [
                x[:, at : at + HALO].reshape(seeds * HALO, width),
                enc_bias[rim : rim + atom_heads * RIM],
                row,
            ]
        )

    def unpack(parcel):
        cut = seeds * HALO
        end = cut + atom_heads * RIM
        return (
            parcel[:cut].reshape(seeds, HALO, width),
            parcel[cut:end],
            parcel[end, :RIM].astype(jnp.int32),
        )

    lower, upper = exchange(parcel(atoms - HALO, atoms - RIM), parcel(0, 0))
    lower_x, lower_bias, lower_index = unpack(lower)
    upper_x, upper_bias, upper_index = unpack(upper)
    x_ext = jnp.concatenate([lower_x, x, upper_x], axis=1)
    bias_ext = jnp.concatenate([lower_bias, enc_bias, upper_bias])
    lower_index = jnp.where(tok == 0, MISSING, lower_index - tokens)
    upper_index = jnp.where(tok == count - 1, MISSING, upper_index + tokens)
    index_ext = jnp.concatenate([lower_index, relative, upper_index])[None]
    rows = atoms + 2 * RIM

    encoded, residual, normed = pl.pallas_call(
        functools.partial(encode_kernel, count),
        out_shape=(
            jax.ShapeDtypeStruct((seeds, rows, width), BF),
            jax.ShapeDtypeStruct((seeds, tokens, token_width), F32),
            jax.ShapeDtypeStruct((seeds, tokens, token_width), BF),
        ),
        scratch_shapes=[
            pltpu.VMEM((seeds, atoms + 2 * HALO, 3 * width), BF),
            pltpu.VMEM((seeds, rows, width), BF),
        ],
        compiler_params=PARAMS,
        name="encode",
    )(x_ext, bias_ext, index_ext, token_cond, enc_project, enc_mix, pool_weight)

    everyone = lax.all_gather(normed, "tok", axis=0)
    vmem = pl.BlockSpec(memory_space=pltpu.VMEM)
    hbm = pl.BlockSpec(memory_space=pl.ANY)
    all_tokens = count * tokens
    state, spread = pl.pallas_call(
        token_kernel,
        out_shape=(
            jax.ShapeDtypeStruct((seeds, tokens, token_width), BF),
            jax.ShapeDtypeStruct((seeds, tokens, width), BF),
        ),
        in_specs=[vmem, vmem, hbm, vmem, vmem, hbm, hbm, hbm, vmem],
        scratch_shapes=[
            pltpu.VMEM((seeds, all_tokens, 2 * token_width), BF),
            pltpu.VMEM((seeds, tokens, token_width), BF),
            pltpu.VMEM((seeds * tokens, token_width), F32),
            pltpu.VMEM((seeds, tokens, token_width), F32),
            pltpu.VMEM(whole_bias.shape, BF),
            pltpu.VMEM(token_mix.shape, BF),
            pltpu.VMEM(swiglu_in.shape, BF),
            pltpu.VMEM(swiglu_out.shape, BF),
            pltpu.SemaphoreType.DMA((4,)),
        ],
        compiler_params=PARAMS,
        name="token",
    )(normed, everyone, whole_bias, residual, token_project, token_mix, swiglu_in, swiglu_out,
      spread_weight)

    low_rows, high_rows = exchange(spread[:, tokens - EDGE :], spread[:, :EDGE])
    spread_ext = jnp.concatenate([low_rows, spread, high_rows], axis=1)
    update = pl.pallas_call(
        functools.partial(decode_kernel, count),
        out_shape=jax.ShapeDtypeStruct((seeds, atoms, width), BF),
        scratch_shapes=[
            pltpu.VMEM((seeds, rows, width), BF),
            pltpu.VMEM((seeds, rows, 3 * width), BF),
            pltpu.VMEM((seeds, atoms, width), BF),
        ],
        compiler_params=PARAMS,
        name="decode",
    )(encoded, spread_ext, index_ext, dec_bias, dec_project, dec_mix)
    return state.transpose(1, 0, 2), update.transpose(1, 0, 2)


def solution(mesh):
    placed = (
        P("tok", "seed", None),
        P("tok"),
        P("tok", None),
        P("seed", "tok", None),
        P("tok", None, None),
        P("tok", None, None),
    ) + (P(),) * 10
    return jax.shard_map(
        per_device,
        mesh=mesh,
        in_specs=placed,
        out_specs=(P("tok", "seed", None), P("tok", "seed", None)),
        check_vma=False,
    )
```

```python
import functools

import jax
import jax.numpy as jnp
from jax import lax
from jax.experimental import pallas as pl
from jax.experimental.pallas import tpu as pltpu
from jax.sharding import PartitionSpec as P

HEADS = 16
QUERY_BLOCK = 32
EPS = 1e-05
NEGATIVE = -1000000000.0
HALO = 128
RIM = 64
EDGE = 8
MISSING = -1000
BF = jnp.bfloat16
F32 = jnp.float32


def layer_norm(values):
    centre = values - jnp.mean(values, axis=-1, keepdims=True)
    variance = jnp.mean(centre * centre, axis=-1, keepdims=True)
    return centre * lax.rsqrt(variance + EPS)


def mm(a, b):
    return jnp.dot(a, b, preferred_element_type=F32)


def mm_t(a, b):
    return lax.dot_general(a, b, (((1,), (1,)), ((), ())), preferred_element_type=F32)


def iota(shape, dim):
    return lax.broadcasted_iota(jnp.int32, shape, dim)


def window_attention(packed, bias, mixed, blocks, key_base, low, high, group):
    seeds, _, quad = packed.shape
    width = quad // 4
    window = bias.shape[1]
    heads = bias.shape[0] // mixed.shape[1]
    size = width // heads
    rows = QUERY_BLOCK * heads
    margin = (window - QUERY_BLOCK) // 2
    column = iota((QUERY_BLOCK, width), 1) // size
    lane = iota((rows, window), 1)

    def step(i, carry):
        scores, places = [], []
        for g in range(group):
            j = i * group + g
            start = pl.multiple_of(key_base + QUERY_BLOCK * j, 16)
            term = bias[pl.ds(pl.multiple_of(rows * j, rows), rows), :].astype(F32)
            spot = lane + start
            term = jnp.where((spot >= low) & (spot < high), term, NEGATIVE)
            for s in range(seeds):
                query = packed[s, pl.ds(pl.multiple_of(start + margin, 16), QUERY_BLOCK), :width]
                query = jnp.concatenate(
                    [jnp.where(column == h, query, jnp.zeros_like(query)) for h in range(heads)]
                )
                keys = packed[s, pl.ds(start, window), width : 2 * width]
                scores.append(mm_t(query, keys) * size ** (-0.5) + term)
                places.append((s, j, start))
        weights = [
            jnp.exp(part - jnp.max(part, axis=-1, keepdims=True)).astype(BF) for part in scores
        ]
        sums = [
            mm(part, packed[s, pl.ds(start, window), 2 * width :])
            for part, (s, _, start) in zip(weights, places)
        ]
        for part, (s, j, _) in zip(sums, places):
            part = part[:, :width] / part[:, width:]
            total = part[:QUERY_BLOCK]
            for h in range(1, heads):
                total = jnp.where(column == h, part[QUERY_BLOCK * h : QUERY_BLOCK * (h + 1)], total)
            first = pl.multiple_of(QUERY_BLOCK * j, QUERY_BLOCK)
            mixed[s, pl.ds(first, QUERY_BLOCK), :] = total.astype(BF)
        return carry

    lax.fori_loop(0, blocks // group, step, 0)


def limits(tok, count, front, inner, total):
    low = jnp.where(tok == 0, front, 0)
    high = jnp.where(tok == count - 1, front + inner, total)
    return low, high


def encode(low, high, x, bias, index, cond, project, mix, pool, enc, residual, packed, mixed):
    seeds, total, width = x.shape
    rows = mixed.shape[1]
    for s in range(seeds):
        for at in range(0, total, 256):
            part = layer_norm(x[s, at : at + 256, :].astype(F32)).astype(BF)
            packed[s, at : at + 256, : 3 * width] = mm(part, project[...]).astype(BF)
    packed[:, :, 3 * width :] = jnp.ones((seeds, total, width), BF)
    window_attention(packed, bias, mixed, rows // QUERY_BLOCK, HALO - RIM - 48, low, high, 2)
    tokens = cond.shape[0]
    chosen = index[...] == iota((tokens, rows), 0)
    counts = jnp.sum(chosen.astype(F32), axis=1, keepdims=True)
    chosen = chosen.astype(BF)
    chunk = rows // 3
    for s in range(seeds):
        sums = jnp.zeros(residual.shape[1:], F32)
        for at in range(0, rows, chunk):
            base = x[s, at + HALO - RIM : at + HALO - RIM + chunk, :].astype(F32)
            part = (base + mm(mixed[s, at : at + chunk, :], mix[...])).astype(BF)
            enc[s, at : at + chunk, :] = part
            lifted = jnp.maximum(mm(part, pool[...]), 0.0).astype(BF)
            sums = sums + mm(chosen[:, at : at + chunk], lifted)
        residual[s] = cond[...].astype(F32) + sums / counts


def attend(bias, query, kv, attended):
    seeds, tokens, width = query.shape
    heads = bias.shape[0]
    size = width // heads
    span = 384
    group = span // size

    def step(i, carry):
        s = i // (heads // group)
        g = i % (heads // group)
        left = pl.multiple_of(g * span, 128)
        tiles = [jnp.zeros((tokens, 128), F32) for _ in range(span // 128)]
        for h in range(group):
            first = size * h // 128
            last = (size * h + size - 1) // 128
            wide_here = (last - first + 1) * 128
            lanes = pl.ds(pl.multiple_of(left + first * 128, 128), wide_here)
            spot = iota((tokens, wide_here), 1) + first * 128
            mine = (spot >= size * h) & (spot < size * (h + 1))
            q = query[s, :, lanes]
            q = jnp.where(mine, q, jnp.zeros_like(q))
            keys = kv[s, :, lanes]
            values = kv[s, :, pl.ds(pl.multiple_of(left + width + first * 128, 128), wide_here)]
            scores = mm_t(q, keys) * size ** (-0.5) + bias[g * group + h].astype(F32)
            weights = jnp.exp(scores - jnp.max(scores, axis=-1, keepdims=True))
            sums = jnp.sum(weights, axis=-1, keepdims=True)
            part = jnp.where(mine, mm(weights.astype(BF), values) / sums, 0.0)
            for t in range(first, last + 1):
                tiles[t] = tiles[t] + part[:, (t - first) * 128 : (t - first + 1) * 128]
        for t, tile in enumerate(tiles):
            attended[s, :, pl.ds(pl.multiple_of(left + t * 128, 128), 128)] = tile
        return carry

    lax.fori_loop(0, seeds * (heads // group), step, 0)


def remote(source, target, send, arrive, **place):
    return pltpu.make_async_remote_copy(
        src_ref=source, dst_ref=target, send_sem=send, recv_sem=arrive,
        device_id=place, device_id_type=pl.DeviceIdType.MESH,
    )


def main_kernel(
    count, groups,
    x, atom_bias, index, cond, enc_project, enc_mix, pool, bias_hbm, project_hbm, mix_hbm, wide_hbm,
    down_hbm, spread_w,
    enc, state_out, spread_out,
    packed, mixed, residual, everyone, kv, query, gate, attended, bias, project, mix, wide, down,
    sems, bias_send, bias_recv, right_send, right_recv, left_send, left_recv, twin_send, twin_recv,
):
    tok = lax.axis_index("tok")
    seed = lax.axis_index("seed")
    chips = count // 2
    chip = tok // 2
    twin = tok + 1 - 2 * (tok % 2)
    hops = chips - 1

    barrier = pltpu.get_barrier_semaphore()

    def greet(**place):
        pl.semaphore_signal(
            barrier, inc=1, device_id=place, device_id_type=pl.DeviceIdType.MESH
        )

    greet(tok=twin)
    for k in range(1, groups):
        greet(seed=lax.rem(seed + k, groups))

    @pl.when(chip > 0)
    def _():
        greet(tok=tok - 2)

    @pl.when(chip < chips - 1)
    def _():
        greet(tok=tok + 2)

    has_left = jnp.where(chip > 0, 1, 0)
    has_right = jnp.where(chip < chips - 1, 1, 0)
    pl.semaphore_wait(barrier, groups + has_left + has_right)

    share = bias_hbm.shape[0]
    slot = bias.at[pl.ds(seed * share, share)]
    bias_copies = [
        remote(bias_hbm, slot, bias_send.at[k - 1], bias_recv.at[k - 1],
               seed=lax.rem(seed + k, groups))
        for k in range(1, groups)
    ]
    for copy in bias_copies:
        copy.start()
    loads = [
        pltpu.make_async_copy(source, target, sems.at[i])
        for i, (source, target) in enumerate(
            (
                (bias_hbm, slot), (project_hbm, project), (mix_hbm, mix), (wide_hbm, wide),
                (down_hbm, down),
            )
        )
    ]
    for load in loads:
        load.start()

    seeds, total, _ = x.shape
    inner = mixed.shape[1] - 2 * RIM
    low, high = limits(tok, count, HALO, inner, total)
    encode(low, high, x, atom_bias, index, cond, enc_project, enc_mix, pool, enc, residual, packed, mixed)

    tokens, width = cond.shape
    everyone[tok] = layer_norm(residual[...]).astype(BF)

    def to_right(k):
        piece = everyone.at[tok - 2 * k]
        return remote(piece, piece, right_send.at[k], right_recv.at[k], tok=tok + 2)

    def to_left(k):
        piece = everyone.at[tok + 2 * k]
        return remote(piece, piece, left_send.at[k], left_recv.at[k], tok=tok - 2)

    def to_twin(k):
        piece = everyone.at[tok + 2 * k]
        return remote(piece, piece, twin_send.at[hops + k], twin_recv.at[hops + k], tok=twin)

    @pl.when(chip < chips - 1)
    def _():
        to_right(0).start()

    @pl.when(chip > 0)
    def _():
        to_left(0).start()

    to_twin(0).start()

    loads[1].wait()
    own = everyone[tok].reshape(seeds * tokens, width)
    query[...] = mm(own, project[:, :width]).astype(BF).reshape(seeds, tokens, width)
    gate[...] = jax.nn.sigmoid(mm(own, project[:, 3 * width :]))

    def keys_values(place):
        part = everyone[place].reshape(seeds * tokens, width)
        first = pl.multiple_of(place * tokens, tokens)
        for at in range(0, 2 * width, width):
            piece = mm(part, project[:, width + at : 2 * width + at]).astype(BF)
            kv[:, pl.ds(first, tokens), at : at + width] = piece.reshape(seeds, tokens, width)

    keys_values(tok)
    to_twin(0).wait_recv()
    keys_values(twin)
    for k in range(1, hops + 1):
        from_left = chip - k >= 0
        from_right = chip + k < chips

        @pl.when(from_left)
        def _(k=k):
            to_right(k - 1).wait_recv()
            to_twin(-k).start()
            if k < hops:

                @pl.when(chip < chips - 1)
                def _():
                    to_right(k).start()

        @pl.when(from_right)
        def _(k=k):
            to_left(k - 1).wait_recv()
            to_twin(k).start()
            if k < hops:

                @pl.when(chip > 0)
                def _():
                    to_left(k).start()

        @pl.when(from_left)
        def _(k=k):
            keys_values(tok - 2 * k)

        @pl.when(from_right)
        def _(k=k):
            keys_values(tok + 2 * k)

        @pl.when(from_left)
        def _(k=k):
            to_twin(-k).wait_recv()
            keys_values(twin - 2 * k)

        @pl.when(from_right)
        def _(k=k):
            to_twin(k).wait_recv()
            keys_values(twin + 2 * k)

    loads[0].wait()
    for copy in bias_copies:
        copy.wait()
    attend(bias, query, kv, attended)

    loads[2].wait()
    gated = (attended[...].reshape(seeds * tokens, width) * gate[...]).astype(BF)
    state = residual[...].reshape(seeds * tokens, width) + mm(gated, mix[...])
    part = layer_norm(state).astype(BF)
    loads[3].wait()
    hidden = down.shape[0]
    part = (jax.nn.silu(mm(part, wide[:, :hidden])) * mm(part, wide[:, hidden:])).astype(BF)
    loads[4].wait()
    state = (state + mm(part, down[...])).astype(BF)
    state_out[...] = state.reshape(seeds, tokens, width)
    spread_out[...] = mm(state, spread_w[...]).astype(BF).reshape(spread_out.shape)

    to_twin(0).wait_send()
    for k in range(hops):

        @pl.when((chip - k >= 0) & (chip < chips - 1))
        def _(k=k):
            to_right(k).wait_send()

        @pl.when((chip + k < chips) & (chip > 0))
        def _(k=k):
            to_left(k).wait_send()

        @pl.when(chip - k - 1 >= 0)
        def _(k=k):
            to_twin(-k - 1).wait_send()

        @pl.when(chip + k + 1 < chips)
        def _(k=k):
            to_twin(k + 1).wait_send()


def decode_kernel(count, enc, spread, index, bias, project, mix, out, decoded, packed, mixed):
    seeds, rows, width = enc.shape
    inner = out.shape[1]
    low, high = limits(lax.axis_index("tok"), count, RIM, inner, rows)
    picker = (index[...] == iota((spread.shape[1], rows), 0) - EDGE).astype(BF)
    chunk = rows // 3
    for s in range(seeds):
        for at in range(0, rows, chunk):
            carried = lax.dot_general(
                picker[:, at : at + chunk], spread[s], (((0,), (0,)), ((), ())),
                preferred_element_type=F32,
            )
            part = (enc[s, at : at + chunk, :].astype(F32) + carried).astype(BF)
            decoded[s, at : at + chunk, :] = part
            part = layer_norm(part.astype(F32)).astype(BF)
            packed[s, at : at + chunk, : 3 * width] = mm(part, project[...]).astype(BF)
    packed[:, :, 3 * width :] = jnp.ones((seeds, rows, width), BF)
    window_attention(packed, bias, mixed, inner // QUERY_BLOCK, RIM - 48, low, high, 2)
    for s in range(seeds):
        for at in range(0, inner, 256):
            base = decoded[s, RIM + at : RIM + at + 256, :].astype(F32)
            out[s, at : at + 256, :] = (base + mm(mixed[s, at : at + 256, :], mix[...])).astype(BF)


PARAMS = pltpu.CompilerParams(vmem_limit_bytes=50 * 1024 * 1024)


def exchange(to_above, to_below):
    count = lax.axis_size("tok")
    above = [(i, i + 1) for i in range(count - 1)]
    below = [(target, source) for source, target in above]
    return lax.ppermute(to_above, "tok", above), lax.ppermute(to_below, "tok", below)


def per_device(
    atom_feats, atom_index, token_cond, pair_bias, atom_bias_enc, atom_bias_dec,
    enc_project, enc_mix, pool_weight, token_project, token_mix, swiglu_in, swiglu_out,
    spread_weight, dec_project, dec_mix,
):
    atoms, seeds, width = atom_feats.shape
    tokens, token_width = token_cond.shape
    atom_heads, window = atom_bias_enc.shape[1:]
    count = lax.axis_size("tok")
    tok = lax.axis_index("tok")
    relative = atom_index - tok * tokens
    x = atom_feats.transpose(1, 0, 2)

    def by_head(bias):
        parts = bias.reshape(atoms // QUERY_BLOCK, QUERY_BLOCK, atom_heads, window)
        return parts.transpose(0, 2, 1, 3).reshape(atoms * atom_heads, window)

    enc_bias = by_head(atom_bias_enc)
    dec_bias = by_head(atom_bias_dec)

    def parcel(at, at_rim):
        row = jnp.zeros((8, width), BF).at[0, :RIM].set(relative[at_rim : at_rim + RIM].astype(BF))
        rim = atom_heads * at_rim
        return jnp.concatenate(
            [
                x[:, at : at + HALO].reshape(seeds * HALO, width),
                enc_bias[rim : rim + atom_heads * RIM],
                row,
            ]
        )

    def unpack(parcel):
        cut = seeds * HALO
        end = cut + atom_heads * RIM
        return (
            parcel[:cut].reshape(seeds, HALO, width),
            parcel[cut:end],
            parcel[end, :RIM].astype(jnp.int32),
        )

    lower, upper = exchange(parcel(atoms - HALO, atoms - RIM), parcel(0, 0))
    lower_x, lower_bias, lower_index = unpack(lower)
    upper_x, upper_bias, upper_index = unpack(upper)
    x_ext = jnp.concatenate([lower_x, x, upper_x], axis=1)
    bias_ext = jnp.concatenate([lower_bias, enc_bias, upper_bias])
    lower_index = jnp.where(tok == 0, MISSING, lower_index - tokens)
    upper_index = jnp.where(tok == count - 1, MISSING, upper_index + tokens)
    index_ext = jnp.concatenate([lower_index, relative, upper_index])[None]
    rows = atoms + 2 * RIM

    groups = lax.axis_size("seed")
    hops = max(count // 2 - 1, 1)
    vmem = pl.BlockSpec(memory_space=pltpu.VMEM)
    hbm = pl.BlockSpec(memory_space=pl.ANY)
    flat = (seeds, tokens, token_width)
    dma = pltpu.SemaphoreType.DMA
    encoded, state, spread = pl.pallas_call(
        functools.partial(main_kernel, count, groups),
        out_shape=(
            jax.ShapeDtypeStruct((seeds, rows, width), BF),
            jax.ShapeDtypeStruct(flat, BF),
            jax.ShapeDtypeStruct((seeds, tokens, width), BF),
        ),
        in_specs=[vmem] * 7 + [hbm] * 5 + [vmem],
        scratch_shapes=[
            pltpu.VMEM((seeds, atoms + 2 * HALO, 4 * width), BF),
            pltpu.VMEM((seeds, rows, width), BF),
            pltpu.VMEM(flat, F32),
            pltpu.VMEM((count,) + flat, BF),
            pltpu.VMEM((seeds, count * tokens, 2 * token_width), BF),
            pltpu.VMEM(flat, BF),
            pltpu.VMEM((seeds * tokens, token_width), F32),
            pltpu.VMEM(flat, F32),
            pltpu.VMEM((HEADS,) + pair_bias.shape[1:], BF),
            pltpu.VMEM(token_project.shape, BF),
            pltpu.VMEM(token_mix.shape, BF),
            pltpu.VMEM(swiglu_in.shape, BF),
            pltpu.VMEM(swiglu_out.shape, BF),
            dma((5,)),
            dma((groups - 1,)),
            dma((groups - 1,)),
            dma((hops,)),
            dma((hops,)),
            dma((hops,)),
            dma((hops,)),
            dma((2 * hops + 1,)),
            dma((2 * hops + 1,)),
        ],
        compiler_params=pltpu.CompilerParams(
            vmem_limit_bytes=56 * 1024 * 1024, collective_id=0, has_side_effects=True
        ),
        name="main",
    )(x_ext, bias_ext, index_ext, token_cond, enc_project, enc_mix, pool_weight, pair_bias,
      token_project, token_mix, swiglu_in, swiglu_out, spread_weight)

    low_rows, high_rows = exchange(spread[:, tokens - EDGE :], spread[:, :EDGE])
    spread_ext = jnp.concatenate([low_rows, spread, high_rows], axis=1)
    update = pl.pallas_call(
        functools.partial(decode_kernel, count),
        out_shape=jax.ShapeDtypeStruct((seeds, atoms, width), BF),
        scratch_shapes=[
            pltpu.VMEM((seeds, rows, width), BF),
            pltpu.VMEM((seeds, rows, 4 * width), BF),
            pltpu.VMEM((seeds, atoms, width), BF),
        ],
        compiler_params=PARAMS,
        name="decode",
    )(encoded, spread_ext, index_ext, dec_bias, dec_project, dec_mix)
    return state.transpose(1, 0, 2), update.transpose(1, 0, 2)


def solution(mesh):
    placed = (
        P("tok", "seed", None),
        P("tok"),
        P("tok", None),
        P("seed", "tok", None),
        P("tok", None, None),
        P("tok", None, None),
    ) + (P(),) * 10
    return jax.shard_map(
        per_device,
        mesh=mesh,
        in_specs=placed,
        out_specs=(P("tok", "seed", None), P("tok", "seed", None)),
        check_vma=False,
    )
```

```python
import functools

import jax
import jax.numpy as jnp
from jax import lax
from jax.experimental import pallas as pl
from jax.experimental.pallas import tpu as pltpu
from jax.sharding import PartitionSpec as P

HEADS = 16
QUERY_BLOCK = 32
EPS = 1e-05
NEGATIVE = -1000000000.0
HALO = 128
RIM = 64
EDGE = 16
MISSING = -1000
BF = jnp.bfloat16
F32 = jnp.float32


def layer_norm(values):
    centre = values - jnp.mean(values, axis=-1, keepdims=True)
    variance = jnp.mean(centre * centre, axis=-1, keepdims=True)
    return centre * lax.rsqrt(variance + EPS)


def mm(a, b):
    return jnp.dot(a, b, preferred_element_type=F32)


def mm_t(a, b):
    return lax.dot_general(a, b, (((1,), (1,)), ((), ())), preferred_element_type=F32)


def iota(shape, dim):
    return lax.broadcasted_iota(jnp.int32, shape, dim)


def window_attention(packed, bias, mixed, first_row, blocks, low, high, group):
    seeds, _, quad = packed.shape
    width = quad // 4
    window = bias.shape[1]
    heads = bias.shape[0] // (QUERY_BLOCK * blocks)
    size = width // heads
    rows = QUERY_BLOCK * heads
    margin = (window - QUERY_BLOCK) // 2
    column = iota((QUERY_BLOCK, width), 1) // size
    lane = iota((rows, window), 1)

    def step(i, carry):
        scores, places = [], []
        for g in range(group):
            j = i * group + g
            start = pl.multiple_of(first_row - margin + QUERY_BLOCK * j, 16)
            term = bias[pl.ds(pl.multiple_of(rows * j, rows), rows), :].astype(F32)
            spot = lane + start
            term = jnp.where((spot >= low) & (spot < high), term, NEGATIVE)
            for s in range(seeds):
                query = packed[s, pl.ds(pl.multiple_of(start + margin, 16), QUERY_BLOCK), :width]
                query = jnp.concatenate(
                    [jnp.where(column == h, query, jnp.zeros_like(query)) for h in range(heads)]
                )
                keys = packed[s, pl.ds(start, window), width : 2 * width]
                scores.append(mm_t(query, keys) * size ** (-0.5) + term)
                places.append((s, j, start))
        weights = [
            jnp.exp(part - jnp.max(part, axis=-1, keepdims=True)).astype(BF) for part in scores
        ]
        sums = [
            mm(part, packed[s, pl.ds(start, window), 2 * width :])
            for part, (s, _, start) in zip(weights, places)
        ]
        for part, (s, j, _) in zip(sums, places):
            part = part[:, :width] / part[:, width:]
            total = part[:QUERY_BLOCK]
            for h in range(1, heads):
                total = jnp.where(column == h, part[QUERY_BLOCK * h : QUERY_BLOCK * (h + 1)], total)
            first = pl.multiple_of(first_row + QUERY_BLOCK * j, QUERY_BLOCK)
            mixed[s, pl.ds(first, QUERY_BLOCK), :] = total.astype(BF)
        return carry

    lax.fori_loop(0, blocks // group, step, 0)


def packed_rows(packed, project, source, begin, end, chunk):
    seeds, _, quad = packed.shape
    used = quad // 4 * 3
    for s in range(seeds):
        for at in range(begin, end, chunk):
            part = layer_norm(source[s, at : at + chunk, :].astype(F32)).astype(BF)
            packed[s, at : at + chunk, :used] = mm(part, project[...]).astype(BF)


def pool_tokens(x, index, cond, mix, pool, enc, residual, mixed):
    seeds, total, width = x.shape
    tokens = cond.shape[0]
    chosen = index == iota((tokens, total), 0)
    counts = jnp.sum(chosen.astype(F32), axis=1, keepdims=True)
    chosen = chosen.astype(BF)
    for s in range(seeds):
        sums = jnp.zeros(residual.shape[1:], F32)
        for at in range(0, total, 256):
            base = x[s, at : at + 256, :].astype(F32)
            part = (base + mm(mixed[s, at : at + 256, :], mix[...])).astype(BF)
            enc[s, at : at + 256, :] = part
            lifted = jnp.maximum(mm(part, pool[...]), 0.0).astype(BF)
            sums = sums + mm(chosen[:, at : at + 256], lifted)
        residual[s] = cond[...].astype(F32) + sums / counts


def attend(bias, query, kv, attended):
    seeds, tokens, width = query.shape
    heads = bias.shape[0]
    size = width // heads
    span = 384
    group = span // size

    def step(i, carry):
        s = i // (heads // group)
        g = i % (heads // group)
        left = pl.multiple_of(g * span, 128)
        tiles = [jnp.zeros((tokens, 128), F32) for _ in range(span // 128)]
        for h in range(group):
            first = size * h // 128
            last = (size * h + size - 1) // 128
            wide_here = (last - first + 1) * 128
            lanes = pl.ds(pl.multiple_of(left + first * 128, 128), wide_here)
            spot = iota((tokens, wide_here), 1) + first * 128
            mine = (spot >= size * h) & (spot < size * (h + 1))
            q = query[s, :, lanes]
            q = jnp.where(mine, q, jnp.zeros_like(q))
            keys = kv[s, :, lanes]
            values = kv[s, :, pl.ds(pl.multiple_of(left + width + first * 128, 128), wide_here)]
            scores = mm_t(q, keys) * size ** (-0.5) + bias[g * group + h].astype(F32)
            weights = jnp.exp(scores - jnp.max(scores, axis=-1, keepdims=True))
            sums = jnp.sum(weights, axis=-1, keepdims=True)
            part = jnp.where(mine, mm(weights.astype(BF), values) / sums, 0.0)
            for t in range(first, last + 1):
                tiles[t] = tiles[t] + part[:, (t - first) * 128 : (t - first + 1) * 128]
        for t, tile in enumerate(tiles):
            attended[s, :, pl.ds(pl.multiple_of(left + t * 128, 128), 128)] = tile
        return carry

    lax.fori_loop(0, seeds * (heads // group), step, 0)


def remote(source, target, send, arrive, **place):
    return pltpu.make_async_remote_copy(
        src_ref=source, dst_ref=target, send_sem=send, recv_sem=arrive,
        device_id=place, device_id_type=pl.DeviceIdType.MESH,
    )


def main_kernel(
    count, groups,
    atoms_in, enc_bias_hbm, index_in, first_index, last_index, cond, enc_project, enc_mix, pool,
    bias_hbm, project_hbm, mix_hbm, wide_hbm, down_hbm, spread_w, dec_bias_hbm, dec_project, dec_mix,
    state_out, out,
    x, atom_bias, low_index, high_index, enc, decoded, spread, dec_bias,
    packed, mixed, residual, everyone, kv, query, gate, attended, bias, project, mix, wide, down,
    sems, bias_send, bias_recv, right_send, right_recv, left_send, left_recv, twin_send, twin_recv,
    up_send, up_recv, down_send, down_recv,
):
    tok = lax.axis_index("tok")
    seed = lax.axis_index("seed")
    chips = count // 2
    inner_tokens = cond.shape[0]
    chip = tok // 2
    twin = tok + 1 - 2 * (tok % 2)
    hops = chips - 1

    barrier = pltpu.get_barrier_semaphore()

    def greet(**place):
        pl.semaphore_signal(
            barrier, inc=1, device_id=place, device_id_type=pl.DeviceIdType.MESH
        )

    greet(tok=twin)
    for k in range(1, groups):
        greet(seed=lax.rem(seed + k, groups))

    @pl.when(chip > 0)
    def _():
        greet(tok=tok - 2)

    @pl.when(chip < chips - 1)
    def _():
        greet(tok=tok + 2)

    side = tok - 1 + 2 * (tok % 2)
    has_side = (side >= 0) & (side < count)

    @pl.when(has_side)
    def _():
        greet(tok=side)

    has_left = jnp.where(chip > 0, 1, 0)
    has_right = jnp.where(chip < chips - 1, 1, 0)
    pl.semaphore_wait(barrier, groups + has_left + has_right + jnp.where(has_side, 1, 0))

    seeds, inner, width = atoms_in.shape
    total = inner + 2 * HALO
    heads = enc_bias_hbm.shape[0] // inner
    rim = heads * RIM
    own_bias = heads * inner
    has_below = tok > 0
    has_above = tok < count - 1

    def up(i, source, target):
        return remote(source, target, up_send.at[i], up_recv.at[i], tok=tok + 1)

    def below(i, source, target):
        return remote(source, target, down_send.at[i], down_recv.at[i], tok=tok - 1)

    upward = [
        (0, atoms_in.at[:, pl.ds(inner - HALO, HALO)], x.at[:, pl.ds(0, HALO)]),
        (1, enc_bias_hbm.at[pl.ds(own_bias - rim, rim)], atom_bias.at[pl.ds(0, rim)]),
        (2, last_index, low_index),
    ]
    downward = [
        (0, atoms_in.at[:, pl.ds(0, HALO)], x.at[:, pl.ds(HALO + inner, HALO)]),
        (1, enc_bias_hbm.at[pl.ds(0, rim)], atom_bias.at[pl.ds(rim + own_bias, rim)]),
        (2, first_index, high_index),
    ]
    edge_up = (3, spread.at[:, pl.ds(inner_tokens, EDGE)], spread.at[:, pl.ds(0, EDGE)])
    edge_down = (3, spread.at[:, pl.ds(EDGE, EDGE)], spread.at[:, pl.ds(EDGE + inner_tokens, EDGE)])

    @pl.when(has_above)
    def _():
        for part in upward:
            up(*part).start()

    @pl.when(has_below)
    def _():
        for part in downward:
            below(*part).start()

    @pl.when(tok == 0)
    def _():
        x[:, :HALO] = jnp.zeros((seeds, HALO, width), BF)
        atom_bias[:rim] = jnp.zeros((rim, width), BF)
        low_index[...] = jnp.full(low_index.shape, MISSING, jnp.int32)
        spread[:, :EDGE] = jnp.zeros((seeds, EDGE, width), BF)

    @pl.when(tok == count - 1)
    def _():
        x[:, HALO + inner :] = jnp.zeros((seeds, HALO, width), BF)
        atom_bias[rim + own_bias :] = jnp.zeros((rim, width), BF)
        high_index[...] = jnp.full(high_index.shape, MISSING, jnp.int32)
        spread[:, EDGE + inner_tokens :] = jnp.zeros((seeds, EDGE, width), BF)

    share = bias_hbm.shape[0]
    slot = bias.at[pl.ds(seed * share, share)]
    bias_copies = [
        remote(bias_hbm, slot, bias_send.at[k - 1], bias_recv.at[k - 1],
               seed=lax.rem(seed + k, groups))
        for k in range(1, groups)
    ]
    for copy in bias_copies:
        copy.start()
    loads = [
        pltpu.make_async_copy(source, target, sems.at[i])
        for i, (source, target) in enumerate(
            (
                (bias_hbm, slot), (project_hbm, project), (mix_hbm, mix), (wide_hbm, wide),
                (down_hbm, down), (dec_bias_hbm, dec_bias),
                (enc_bias_hbm, atom_bias.at[pl.ds(rim, own_bias)]),
            )
        )
    ]
    for load in loads:
        load.start()

    x[:, HALO : HALO + inner] = atoms_in[...]
    packed[:, :, 3 * width :] = jnp.ones((seeds, total, width), BF)
    mixed[:, :RIM] = jnp.zeros((seeds, RIM, width), BF)
    mixed[:, total - RIM :] = jnp.zeros((seeds, RIM, width), BF)
    packed_rows(packed, enc_project, x, HALO, HALO + inner, 256)

    @pl.when(has_below)
    def _():
        for part in upward:
            up(*part).wait_recv()

    @pl.when(has_above)
    def _():
        for part in downward:
            below(*part).wait_recv()

    packed_rows(packed, enc_project, x, 0, HALO, HALO)
    packed_rows(packed, enc_project, x, HALO + inner, total, HALO)
    low = jnp.where(tok == 0, HALO, 0)
    high = jnp.where(tok == count - 1, HALO + inner, total)
    loads[6].wait()
    blocks = inner // QUERY_BLOCK
    rim_blocks = 2 * RIM // QUERY_BLOCK
    window_attention(packed, atom_bias, mixed, HALO - RIM, blocks + rim_blocks, low, high, 2)
    index = jnp.concatenate([low_index[:1], index_in[...], high_index[:1]], axis=1)
    index = index - tok * inner_tokens
    pool_tokens(x, index, cond, enc_mix, pool, enc, residual, mixed)

    tokens, width = cond.shape
    everyone[tok] = layer_norm(residual[...]).astype(BF)

    def to_right(k):
        piece = everyone.at[tok - 2 * k]
        return remote(piece, piece, right_send.at[k], right_recv.at[k], tok=tok + 2)

    def to_left(k):
        piece = everyone.at[tok + 2 * k]
        return remote(piece, piece, left_send.at[k], left_recv.at[k], tok=tok - 2)

    def to_twin(k):
        piece = everyone.at[tok + 2 * k]
        return remote(piece, piece, twin_send.at[hops + k], twin_recv.at[hops + k], tok=twin)

    @pl.when(chip < chips - 1)
    def _():
        to_right(0).start()

    @pl.when(chip > 0)
    def _():
        to_left(0).start()

    to_twin(0).start()

    loads[1].wait()
    own = everyone[tok].reshape(seeds * tokens, width)
    query[...] = mm(own, project[:, :width]).astype(BF).reshape(seeds, tokens, width)
    gate[...] = jax.nn.sigmoid(mm(own, project[:, 3 * width :]))

    def keys_values(place):
        part = everyone[place].reshape(seeds * tokens, width)
        first = pl.multiple_of(place * tokens, tokens)
        for at in range(0, 2 * width, width):
            piece = mm(part, project[:, width + at : 2 * width + at]).astype(BF)
            kv[:, pl.ds(first, tokens), at : at + width] = piece.reshape(seeds, tokens, width)

    keys_values(tok)
    to_twin(0).wait_recv()
    keys_values(twin)
    for k in range(1, hops + 1):
        from_left = chip - k >= 0
        from_right = chip + k < chips

        @pl.when(from_left)
        def _(k=k):
            to_right(k - 1).wait_recv()
            to_twin(-k).start()
            if k < hops:

                @pl.when(chip < chips - 1)
                def _():
                    to_right(k).start()

        @pl.when(from_right)
        def _(k=k):
            to_left(k - 1).wait_recv()
            to_twin(k).start()
            if k < hops:

                @pl.when(chip > 0)
                def _():
                    to_left(k).start()

        @pl.when(from_left)
        def _(k=k):
            keys_values(tok - 2 * k)

        @pl.when(from_right)
        def _(k=k):
            keys_values(tok + 2 * k)

        @pl.when(from_left)
        def _(k=k):
            to_twin(-k).wait_recv()
            keys_values(twin - 2 * k)

        @pl.when(from_right)
        def _(k=k):
            to_twin(k).wait_recv()
            keys_values(twin + 2 * k)

    loads[0].wait()
    for copy in bias_copies:
        copy.wait()
    attend(bias, query, kv, attended)

    loads[2].wait()
    gated = (attended[...].reshape(seeds * tokens, width) * gate[...]).astype(BF)
    state = residual[...].reshape(seeds * tokens, width) + mm(gated, mix[...])
    part = layer_norm(state).astype(BF)
    loads[3].wait()
    hidden = down.shape[0]
    part = (jax.nn.silu(mm(part, wide[:, :hidden])) * mm(part, wide[:, hidden:])).astype(BF)
    loads[4].wait()
    state = (state + mm(part, down[...])).astype(BF)
    state_out[...] = state.reshape(seeds, tokens, width)
    part = mm(state, spread_w[...]).astype(BF)
    spread[:, EDGE : EDGE + tokens] = part.reshape(seeds, tokens, part.shape[1])

    @pl.when(has_above)
    def _():
        up(*edge_up).start()

    @pl.when(has_below)
    def _():
        below(*edge_down).start()

    @pl.when(has_below)
    def _():
        up(*edge_up).wait_recv()

    @pl.when(has_above)
    def _():
        below(*edge_down).wait_recv()

    picker = (index == iota((tokens + 2 * EDGE, total), 0) - EDGE).astype(BF)
    for s in range(seeds):
        for at in range(0, total, 256):
            carried = lax.dot_general(
                picker[:, at : at + 256], spread[s], (((0,), (0,)), ((), ())),
                preferred_element_type=F32,
            )
            decoded[s, at : at + 256, :] = (
                enc[s, at : at + 256, :].astype(F32) + carried
            ).astype(BF)
    packed_rows(packed, dec_project, decoded, 0, total, 256)
    loads[5].wait()
    window_attention(packed, dec_bias, mixed, HALO, blocks, low, high, 2)
    for s in range(seeds):
        for at in range(HALO, HALO + inner, 256):
            base = decoded[s, at : at + 256, :].astype(F32)
            part = base + mm(mixed[s, at : at + 256, :], dec_mix[...])
            out[s, at - HALO : at - HALO + 256, :] = part.astype(BF)

    @pl.when(has_above)
    def _():
        for part in upward + [edge_up]:
            up(*part).wait_send()

    @pl.when(has_below)
    def _():
        for part in downward + [edge_down]:
            below(*part).wait_send()

    to_twin(0).wait_send()
    for k in range(hops):

        @pl.when((chip - k >= 0) & (chip < chips - 1))
        def _(k=k):
            to_right(k).wait_send()

        @pl.when((chip + k < chips) & (chip > 0))
        def _(k=k):
            to_left(k).wait_send()

        @pl.when(chip - k - 1 >= 0)
        def _(k=k):
            to_twin(-k - 1).wait_send()

        @pl.when(chip + k + 1 < chips)
        def _(k=k):
            to_twin(k + 1).wait_send()


def per_device(
    atom_feats, atom_index, token_cond, pair_bias, atom_bias_enc, atom_bias_dec,
    enc_project, enc_mix, pool_weight, token_project, token_mix, swiglu_in, swiglu_out,
    spread_weight, dec_project, dec_mix,
):
    atoms, seeds, width = atom_feats.shape
    tokens, token_width = token_cond.shape
    atom_heads, window = atom_bias_enc.shape[1:]
    count = lax.axis_size("tok")
    x = atom_feats.transpose(1, 0, 2)

    def by_head(bias):
        parts = bias.reshape(atoms // QUERY_BLOCK, QUERY_BLOCK, atom_heads, window)
        return parts.transpose(0, 2, 1, 3).reshape(atoms * atom_heads, window)

    enc_bias = by_head(atom_bias_enc)
    dec_bias = by_head(atom_bias_dec)

    first_index = jnp.broadcast_to(atom_index[None, :HALO], (8, HALO))
    last_index = jnp.broadcast_to(atom_index[None, atoms - HALO :], (8, HALO))
    total = atoms + 2 * HALO
    groups = lax.axis_size("seed")
    hops = max(count // 2 - 1, 1)
    vmem = pl.BlockSpec(memory_space=pltpu.VMEM)
    hbm = pl.BlockSpec(memory_space=pl.ANY)
    flat = (seeds, tokens, token_width)
    dma = pltpu.SemaphoreType.DMA
    state, update = pl.pallas_call(
        functools.partial(main_kernel, count, groups),
        out_shape=(
            jax.ShapeDtypeStruct(flat, BF),
            jax.ShapeDtypeStruct((seeds, atoms, width), BF),
        ),
        in_specs=[vmem, hbm] + [vmem] * 7 + [hbm] * 5 + [vmem, hbm, vmem, vmem],
        scratch_shapes=[
            pltpu.VMEM((seeds, total, width), BF),
            pltpu.VMEM(((atoms + 2 * RIM) * atom_heads, window), BF),
            pltpu.VMEM((8, HALO), jnp.int32),
            pltpu.VMEM((8, HALO), jnp.int32),
            pltpu.VMEM((seeds, total, width), BF),
            pltpu.VMEM((seeds, total, width), BF),
            pltpu.VMEM((seeds, tokens + 2 * EDGE, width), BF),
            pltpu.VMEM(dec_bias.shape, BF),
            pltpu.VMEM((seeds, total, 4 * width), BF),
            pltpu.VMEM((seeds, total, width), BF),
            pltpu.VMEM(flat, F32),
            pltpu.VMEM((count,) + flat, BF),
            pltpu.VMEM((seeds, count * tokens, 2 * token_width), BF),
            pltpu.VMEM(flat, BF),
            pltpu.VMEM((seeds * tokens, token_width), F32),
            pltpu.VMEM(flat, F32),
            pltpu.VMEM((HEADS,) + pair_bias.shape[1:], BF),
            pltpu.VMEM(token_project.shape, BF),
            pltpu.VMEM(token_mix.shape, BF),
            pltpu.VMEM(swiglu_in.shape, BF),
            pltpu.VMEM(swiglu_out.shape, BF),
            dma((7,)),
            dma((groups - 1,)),
            dma((groups - 1,)),
            dma((hops,)),
            dma((hops,)),
            dma((hops,)),
            dma((hops,)),
            dma((2 * hops + 1,)),
            dma((2 * hops + 1,)),
            dma((4,)),
            dma((4,)),
            dma((4,)),
            dma((4,)),
        ],
        compiler_params=pltpu.CompilerParams(
            vmem_limit_bytes=60 * 1024 * 1024, collective_id=0, has_side_effects=True
        ),
        name="main",
    )(x, enc_bias, atom_index[None], first_index, last_index, token_cond, enc_project, enc_mix,
      pool_weight, pair_bias, token_project, token_mix, swiglu_in, swiglu_out, spread_weight,
      dec_bias, dec_project, dec_mix)
    return state.transpose(1, 0, 2), update.transpose(1, 0, 2)


def solution(mesh):
    placed = (
        P("tok", "seed", None),
        P("tok"),
        P("tok", None),
        P("seed", "tok", None),
        P("tok", None, None),
        P("tok", None, None),
    ) + (P(),) * 10
    return jax.shard_map(
        per_device,
        mesh=mesh,
        in_specs=placed,
        out_specs=(P("tok", "seed", None), P("tok", "seed", None)),
        check_vma=False,
    )
```

```python
import functools

import jax
import jax.numpy as jnp
from jax import lax
from jax.experimental import pallas as pl
from jax.experimental.pallas import tpu as pltpu
from jax.sharding import PartitionSpec as P

HEADS = 16
QUERY_BLOCK = 32
EPS = 1e-05
NEGATIVE = -1000000000.0
HALO = 128
RIM = 64
EDGE = 16
MISSING = -1000
BF = jnp.bfloat16
F32 = jnp.float32


def layer_norm(values):
    centre = values - jnp.mean(values, axis=-1, keepdims=True)
    variance = jnp.mean(centre * centre, axis=-1, keepdims=True)
    return centre * lax.rsqrt(variance + EPS)


def mm(a, b):
    return jnp.dot(a, b, preferred_element_type=F32)


def mm_t(a, b):
    return lax.dot_general(a, b, (((1,), (1,)), ((), ())), preferred_element_type=F32)


def iota(shape, dim):
    return lax.broadcasted_iota(jnp.int32, shape, dim)


def window_attention(packed, bias, mixed, first_row, blocks, low, high, group):
    seeds, _, quad = packed.shape
    width = quad // 4
    window = bias.shape[1]
    heads = bias.shape[0] // (QUERY_BLOCK * blocks)
    size = width // heads
    rows = QUERY_BLOCK * heads
    margin = (window - QUERY_BLOCK) // 2
    column = iota((QUERY_BLOCK, width), 1) // size
    lane = iota((rows, window), 1)
    row, source = iota((rows, rows), 0), iota((rows, rows), 1)
    order = (source // heads == row % QUERY_BLOCK) & (source % heads == row // QUERY_BLOCK)
    order = order.astype(BF)

    def step(i, carry):
        scores, places = [], []
        for g in range(group):
            j = i * group + g
            start = pl.multiple_of(first_row - margin + QUERY_BLOCK * j, 16)
            term = mm(order, bias[pl.ds(pl.multiple_of(rows * j, rows), rows), :])
            spot = lane + start
            term = jnp.where((spot >= low) & (spot < high), term, NEGATIVE)
            for s in range(seeds):
                query = packed[s, pl.ds(pl.multiple_of(start + margin, 16), QUERY_BLOCK), :width]
                query = jnp.concatenate(
                    [jnp.where(column == h, query, jnp.zeros_like(query)) for h in range(heads)]
                )
                keys = packed[s, pl.ds(start, window), width : 2 * width]
                scores.append(mm_t(query, keys) * size ** (-0.5) + term)
                places.append((s, j, start))
        weights = [
            jnp.exp(part - jnp.max(part, axis=-1, keepdims=True)).astype(BF) for part in scores
        ]
        sums = [
            mm(part, packed[s, pl.ds(start, window), 2 * width :])
            for part, (s, _, start) in zip(weights, places)
        ]
        for part, (s, j, _) in zip(sums, places):
            part = part[:, :width] / part[:, width:]
            total = part[:QUERY_BLOCK]
            for h in range(1, heads):
                total = jnp.where(column == h, part[QUERY_BLOCK * h : QUERY_BLOCK * (h + 1)], total)
            first = pl.multiple_of(first_row + QUERY_BLOCK * j, QUERY_BLOCK)
            mixed[s, pl.ds(first, QUERY_BLOCK), :] = total.astype(BF)
        return carry

    lax.fori_loop(0, blocks // group, step, 0)


def packed_rows(packed, project, source, begin, end, chunk):
    seeds, _, quad = packed.shape
    used = quad // 4 * 3
    for s in range(seeds):
        for at in range(begin, end, chunk):
            part = layer_norm(source[s, at : at + chunk, :].astype(F32)).astype(BF)
            packed[s, at : at + chunk, :used] = mm(part, project[...]).astype(BF)


def pool_tokens(x, index, cond, mix, pool, enc, residual, mixed):
    seeds, total, width = x.shape
    tokens = cond.shape[0]
    chosen = index == iota((tokens, total), 0)
    counts = jnp.sum(chosen.astype(F32), axis=1, keepdims=True)
    chosen = chosen.astype(BF)
    for s in range(seeds):
        sums = jnp.zeros(residual.shape[1:], F32)
        for at in range(0, total, 256):
            base = x[s, at : at + 256, :].astype(F32)
            part = (base + mm(mixed[s, at : at + 256, :], mix[...])).astype(BF)
            enc[s, at : at + 256, :] = part
            lifted = jnp.maximum(mm(part, pool[...]), 0.0).astype(BF)
            sums = sums + mm(chosen[:, at : at + 256], lifted)
        residual[s] = cond[...].astype(F32) + sums / counts


def head_lanes(size, h, rows):
    first = size * h // 128
    last = (size * h + size - 1) // 128
    spot = iota((rows, (last - first + 1) * 128), 1) + first * 128
    return first, last, (spot >= size * h) & (spot < size * (h + 1))


def attend(first_key, bias, query, kv, attended, tops, sums):
    seeds, tokens, width = query.shape
    keys_here = 2 * tokens
    heads = bias.shape[0]
    size = width // heads
    span = 384
    group = span // size
    where = pl.ds(pl.multiple_of(first_key, keys_here), keys_here)

    def step(i, carry):
        s = i // (heads // group)
        g = i % (heads // group)
        left = pl.multiple_of(g * span, 128)
        tiles = [
            attended[s, :, pl.ds(pl.multiple_of(left + t * 128, 128), 128)]
            for t in range(span // 128)
        ]
        for h in range(group):
            first, last, mine = head_lanes(size, h, tokens)
            wide = (last - first + 1) * 128
            lanes = pl.ds(pl.multiple_of(left + first * 128, 128), wide)
            q = query[s, :, lanes]
            q = jnp.where(mine, q, jnp.zeros_like(q))
            keys = kv[:, s, :, lanes].reshape(keys_here, wide)
            values = kv[:, s, :, pl.ds(pl.multiple_of(left + width + first * 128, 128), wide)]
            scores = mm_t(q, keys) * size ** (-0.5) + bias[g * group + h, :, where].astype(F32)
            spot = s * heads + g * group + h
            before = tops[spot]
            top = jnp.maximum(before, jnp.max(scores, axis=-1, keepdims=True))
            shrink = jnp.exp(before - top)
            weights = jnp.exp(scores - jnp.concatenate([top] * (keys_here // 128), axis=1))
            total = sums[spot] * shrink
            for at in range(0, keys_here, 128):
                total = total + weights[:, at : at + 128]
            tops[spot] = top
            sums[spot] = total
            part = mm(weights.astype(BF), values.reshape(keys_here, wide))
            for t in range(first, last + 1):
                here = slice((t - first) * 128, (t - first + 1) * 128)
                tiles[t] = jnp.where(mine[:, here], tiles[t] * shrink + part[:, here], tiles[t])
        for t, tile in enumerate(tiles):
            attended[s, :, pl.ds(pl.multiple_of(left + t * 128, 128), 128)] = tile
        return carry

    lax.fori_loop(0, seeds * (heads // group), step, 0)


def settle(heads, attended, sums):
    seeds, tokens, width = attended.shape
    size = width // heads
    span = 384
    group = span // size

    def step(i, carry):
        s = i // (heads // group)
        g = i % (heads // group)
        tiles = [jnp.ones((tokens, 128), F32) for _ in range(span // 128)]
        for h in range(group):
            first, last, mine = head_lanes(size, h, tokens)
            total = jnp.sum(sums[s * heads + g * group + h], axis=-1, keepdims=True)
            for t in range(first, last + 1):
                here = slice((t - first) * 128, (t - first + 1) * 128)
                tiles[t] = jnp.where(mine[:, here], total, tiles[t])
        for t, tile in enumerate(tiles):
            lanes = pl.ds(pl.multiple_of(g * span + t * 128, 128), 128)
            attended[s, :, lanes] = attended[s, :, lanes] / tile
        return carry

    lax.fori_loop(0, seeds * (heads // group), step, 0)


def remote(source, target, send, arrive, **place):
    return pltpu.make_async_remote_copy(
        src_ref=source, dst_ref=target, send_sem=send, recv_sem=arrive,
        device_id=place, device_id_type=pl.DeviceIdType.MESH,
    )


def main_kernel(
    count, groups,
    atoms_in, enc_bias_hbm, index_in, cond, enc_project, enc_mix, pool,
    bias_hbm, project_hbm, mix_hbm, wide_hbm, down_hbm, spread_w, dec_bias_hbm, dec_project, dec_mix,
    state_out, out,
    x, atom_bias, low_index, high_index, enc, decoded, spread, dec_bias,
    packed, mixed, residual, everyone, kv, query, gate, attended, tops, sums, bias, project, mix, wide, down,
    sems, bias_send, bias_recv, right_send, right_recv, left_send, left_recv, twin_send, twin_recv,
    up_send, up_recv, down_send, down_recv,
):
    tok = lax.axis_index("tok")
    seed = lax.axis_index("seed")
    chips = count // 2
    inner_tokens = cond.shape[0]
    chip = tok // 2
    twin = tok + 1 - 2 * (tok % 2)
    hops = chips - 1

    barrier = pltpu.get_barrier_semaphore()

    def greet(**place):
        pl.semaphore_signal(
            barrier, inc=1, device_id=place, device_id_type=pl.DeviceIdType.MESH
        )

    greet(tok=twin)
    for k in range(1, groups):
        greet(seed=lax.rem(seed + k, groups))

    @pl.when(chip > 0)
    def _():
        greet(tok=tok - 2)

    @pl.when(chip < chips - 1)
    def _():
        greet(tok=tok + 2)

    side = tok - 1 + 2 * (tok % 2)
    has_side = (side >= 0) & (side < count)

    @pl.when(has_side)
    def _():
        greet(tok=side)

    has_left = jnp.where(chip > 0, 1, 0)
    has_right = jnp.where(chip < chips - 1, 1, 0)
    pl.semaphore_wait(barrier, groups + has_left + has_right + jnp.where(has_side, 1, 0))

    seeds, total, width = x.shape
    inner = total - 2 * HALO
    turn = seeds * HALO
    row, source = iota((turn, turn), 0), iota((turn, turn), 1)
    split = (source == seeds * (row % HALO) + row // HALO).astype(BF)

    def take_in(at):
        part = mm(split, atoms_in[seeds * at : seeds * (at + HALO), :]).astype(BF)
        for s in range(seeds):
            x[s, HALO + at : 2 * HALO + at, :] = part[s * HALO : (s + 1) * HALO]

    take_in(0)
    take_in(inner - HALO)
    heads = enc_bias_hbm.shape[0] // inner
    rim = heads * RIM
    own_bias = heads * inner
    has_below = tok > 0
    has_above = tok < count - 1

    def up(i, source, target):
        return remote(source, target, up_send.at[i], up_recv.at[i], tok=tok + 1)

    def below(i, source, target):
        return remote(source, target, down_send.at[i], down_recv.at[i], tok=tok - 1)

    upward = [
        (0, x.at[:, pl.ds(inner, HALO)], x.at[:, pl.ds(0, HALO)]),
        (1, enc_bias_hbm.at[pl.ds(own_bias - rim, rim)], atom_bias.at[pl.ds(0, rim)]),
        (2, index_in, low_index),
    ]
    downward = [
        (0, x.at[:, pl.ds(HALO, HALO)], x.at[:, pl.ds(HALO + inner, HALO)]),
        (1, enc_bias_hbm.at[pl.ds(0, rim)], atom_bias.at[pl.ds(rim + own_bias, rim)]),
        (2, index_in, high_index),
    ]
    edge_up = (3, spread.at[:, pl.ds(inner_tokens, EDGE)], spread.at[:, pl.ds(0, EDGE)])
    edge_down = (3, spread.at[:, pl.ds(EDGE, EDGE)], spread.at[:, pl.ds(EDGE + inner_tokens, EDGE)])

    @pl.when(has_above)
    def _():
        for part in upward:
            up(*part).start()

    @pl.when(has_below)
    def _():
        for part in downward:
            below(*part).start()

    @pl.when(tok == 0)
    def _():
        x[:, :HALO] = jnp.zeros((seeds, HALO, width), BF)
        atom_bias[:rim] = jnp.zeros((rim, width), BF)
        low_index[...] = jnp.full(low_index.shape, MISSING, jnp.int32)
        spread[:, :EDGE] = jnp.zeros((seeds, EDGE, width), BF)

    @pl.when(tok == count - 1)
    def _():
        x[:, HALO + inner :] = jnp.zeros((seeds, HALO, width), BF)
        atom_bias[rim + own_bias :] = jnp.zeros((rim, width), BF)
        high_index[...] = jnp.full(high_index.shape, MISSING, jnp.int32)
        spread[:, EDGE + inner_tokens :] = jnp.zeros((seeds, EDGE, width), BF)

    share = bias_hbm.shape[0]
    slot = bias.at[pl.ds(seed * share, share)]
    both = jnp.minimum(chip, chips - 1 - chip)

    def offset(p):
        near = (p + 1) // 2
        inside = jnp.where(p % 2 == 1, -near, near)
        outside = jnp.where(chip > chips - 1 - chip, both - p, p - both)
        return jnp.where(p <= 2 * both, inside, outside)

    def event(k):
        return jnp.where(k <= both + 1, max(1, 2 * (k - 1)), both + k)

    def bias_copy(k, p):
        first = pl.multiple_of((chip + offset(p)) * (2 * inner_tokens), 2 * inner_tokens)
        lanes = pl.ds(first, 2 * inner_tokens)
        return remote(
            bias_hbm.at[:, :, lanes], bias.at[pl.ds(seed * share, share), :, lanes],
            bias_send.at[k - 1, p], bias_recv.at[k - 1, p], seed=lax.rem(seed + k, groups),
        )

    for p in range(chips):
        for k in range(1, groups):
            bias_copy(k, p).start()
    loads = [
        pltpu.make_async_copy(source, target, sems.at[i])
        for i, (source, target) in enumerate(
            (
                (bias_hbm, slot), (project_hbm, project), (mix_hbm, mix), (wide_hbm, wide),
                (down_hbm, down), (dec_bias_hbm, dec_bias),
                (enc_bias_hbm, atom_bias.at[pl.ds(rim, own_bias)]),
            )
        )
    ]
    for load in loads:
        load.start()

    for at in range(HALO, inner - HALO, HALO):
        take_in(at)
    packed[:, :, 3 * width :] = jnp.ones((seeds, total, width), BF)
    mixed[:, :RIM] = jnp.zeros((seeds, RIM, width), BF)
    mixed[:, total - RIM :] = jnp.zeros((seeds, RIM, width), BF)
    packed_rows(packed, enc_project, x, HALO, HALO + inner, 256)

    @pl.when(has_below)
    def _():
        for part in upward:
            up(*part).wait_recv()

    @pl.when(has_above)
    def _():
        for part in downward:
            below(*part).wait_recv()

    packed_rows(packed, enc_project, x, 0, HALO, HALO)
    packed_rows(packed, enc_project, x, HALO + inner, total, HALO)
    low = jnp.where(tok == 0, HALO, 0)
    high = jnp.where(tok == count - 1, HALO + inner, total)
    loads[6].wait()
    blocks = inner // QUERY_BLOCK
    rim_blocks = 2 * RIM // QUERY_BLOCK
    window_attention(packed, atom_bias, mixed, HALO - RIM, blocks + rim_blocks, low, high, 2)
    index = jnp.concatenate(
        [low_index[inner // HALO - 1 :]]
        + [index_in[i : i + 1] for i in range(inner // HALO)]
        + [high_index[:1]],
        axis=1,
    )
    index = index - tok * inner_tokens
    pool_tokens(x, index, cond, enc_mix, pool, enc, residual, mixed)

    tokens, width = cond.shape
    everyone[tok] = layer_norm(residual[...]).astype(BF)

    def to_right(k):
        piece = everyone.at[tok - 2 * k]
        return remote(piece, piece, right_send.at[k], right_recv.at[k], tok=tok + 2)

    def to_left(k):
        piece = everyone.at[tok + 2 * k]
        return remote(piece, piece, left_send.at[k], left_recv.at[k], tok=tok - 2)

    def to_twin(k):
        piece = everyone.at[tok + 2 * k]
        return remote(piece, piece, twin_send.at[hops + k], twin_recv.at[hops + k], tok=twin)

    @pl.when(chip < chips - 1)
    def _():
        to_right(0).start()

    @pl.when(chip > 0)
    def _():
        to_left(0).start()

    to_twin(0).start()

    loads[1].wait()
    own = everyone[tok].reshape(seeds * tokens, width)
    query[...] = mm(own, project[:, :width]).astype(BF).reshape(seeds, tokens, width)
    gate[...] = jax.nn.sigmoid(mm(own, project[:, 3 * width :]))

    attended[...] = jnp.zeros(attended.shape, F32)
    sums[...] = jnp.zeros(sums.shape, F32)
    tops[...] = jnp.full(tops.shape, NEGATIVE, F32)
    loads[0].wait()

    def visit(p, carry):
        for k in range(1, hops + 1):

            @pl.when((p == event(k)) & (chip - k >= 0))
            def _(k=k):
                to_right(k - 1).wait_recv()
                to_twin(-k).start()
                if k < hops:

                    @pl.when(chip < chips - 1)
                    def _():
                        to_right(k).start()

            @pl.when((p == event(k)) & (chip + k < chips))
            def _(k=k):
                to_left(k - 1).wait_recv()
                to_twin(k).start()
                if k < hops:

                    @pl.when(chip > 0)
                    def _():
                        to_left(k).start()

        away = offset(p)
        to_twin(away).wait_recv()
        part = everyone[pl.ds(2 * (chip + away), 2)].reshape(2 * seeds * tokens, width)
        for at in range(0, 2 * width, width):
            piece = mm(part, project[:, width + at : 2 * width + at]).astype(BF)
            kv[:, :, :, at : at + width] = piece.reshape(2, seeds, tokens, width)
        for k in range(1, groups):
            bias_copy(k, p).wait_recv()
        attend((chip + away) * (2 * tokens), bias, query, kv, attended, tops, sums)
        return carry

    lax.fori_loop(0, chips, visit, 0)
    settle(bias.shape[0], attended, sums)

    loads[2].wait()
    gated = (attended[...].reshape(seeds * tokens, width) * gate[...]).astype(BF)
    state = residual[...].reshape(seeds * tokens, width) + mm(gated, mix[...])
    part = layer_norm(state).astype(BF)
    loads[3].wait()
    hidden = down.shape[0]
    part = (jax.nn.silu(mm(part, wide[:, :hidden])) * mm(part, wide[:, hidden:])).astype(BF)
    loads[4].wait()
    state = (state + mm(part, down[...])).astype(BF)
    state_out[...] = state.reshape(seeds, tokens, width)
    part = mm(state, spread_w[...]).astype(BF)
    spread[:, EDGE : EDGE + tokens] = part.reshape(seeds, tokens, part.shape[1])

    @pl.when(has_above)
    def _():
        up(*edge_up).start()

    @pl.when(has_below)
    def _():
        below(*edge_down).start()

    @pl.when(has_below)
    def _():
        up(*edge_up).wait_recv()

    @pl.when(has_above)
    def _():
        below(*edge_down).wait_recv()

    picker = (index == iota((tokens + 2 * EDGE, total), 0) - EDGE).astype(BF)
    for s in range(seeds):
        for at in range(0, total, 256):
            carried = lax.dot_general(
                picker[:, at : at + 256], spread[s], (((0,), (0,)), ((), ())),
                preferred_element_type=F32,
            )
            decoded[s, at : at + 256, :] = (
                enc[s, at : at + 256, :].astype(F32) + carried
            ).astype(BF)
    packed_rows(packed, dec_project, decoded, 0, total, 256)
    loads[5].wait()
    window_attention(packed, dec_bias, mixed, HALO, blocks, low, high, 2)
    for s in range(seeds):
        for at in range(HALO, HALO + inner, 256):
            base = decoded[s, at : at + 256, :].astype(F32)
            part = base + mm(mixed[s, at : at + 256, :], dec_mix[...])
            out[s, at - HALO : at - HALO + 256, :] = part.astype(BF)

    @pl.when(has_above)
    def _():
        for part in upward + [edge_up]:
            up(*part).wait_send()

    @pl.when(has_below)
    def _():
        for part in downward + [edge_down]:
            below(*part).wait_send()

    to_twin(0).wait_send()
    for p in range(chips):
        for k in range(1, groups):
            bias_copy(k, p).wait_send()
    for k in range(hops):

        @pl.when((chip - k >= 0) & (chip < chips - 1))
        def _(k=k):
            to_right(k).wait_send()

        @pl.when((chip + k < chips) & (chip > 0))
        def _(k=k):
            to_left(k).wait_send()

        @pl.when(chip - k - 1 >= 0)
        def _(k=k):
            to_twin(-k - 1).wait_send()

        @pl.when(chip + k + 1 < chips)
        def _(k=k):
            to_twin(k + 1).wait_send()


def per_device(
    atom_feats, atom_index, token_cond, pair_bias, atom_bias_enc, atom_bias_dec,
    enc_project, enc_mix, pool_weight, token_project, token_mix, swiglu_in, swiglu_out,
    spread_weight, dec_project, dec_mix,
):
    atoms, seeds, width = atom_feats.shape
    tokens, token_width = token_cond.shape
    atom_heads, window = atom_bias_enc.shape[1:]
    count = lax.axis_size("tok")
    x = atom_feats.reshape(atoms * seeds, width)

    enc_bias = atom_bias_enc.reshape(atoms * atom_heads, window)
    dec_bias = atom_bias_dec.reshape(atoms * atom_heads, window)
    index = atom_index.reshape(atoms // HALO, HALO)
    total = atoms + 2 * HALO
    groups = lax.axis_size("seed")
    hops = max(count // 2 - 1, 1)
    vmem = pl.BlockSpec(memory_space=pltpu.VMEM)
    hbm = pl.BlockSpec(memory_space=pl.ANY)
    flat = (seeds, tokens, token_width)
    dma = pltpu.SemaphoreType.DMA
    state, update = pl.pallas_call(
        functools.partial(main_kernel, count, groups),
        out_shape=(
            jax.ShapeDtypeStruct(flat, BF),
            jax.ShapeDtypeStruct((seeds, atoms, width), BF),
        ),
        in_specs=[vmem, hbm] + [vmem] * 5 + [hbm] * 5 + [vmem, hbm, vmem, vmem],
        scratch_shapes=[
            pltpu.VMEM((seeds, total, width), BF),
            pltpu.VMEM(((atoms + 2 * RIM) * atom_heads, window), BF),
            pltpu.VMEM(index.shape, jnp.int32),
            pltpu.VMEM(index.shape, jnp.int32),
            pltpu.VMEM((seeds, total, width), BF),
            pltpu.VMEM((seeds, total, width), BF),
            pltpu.VMEM((seeds, tokens + 2 * EDGE, width), BF),
            pltpu.VMEM(dec_bias.shape, BF),
            pltpu.VMEM((seeds, total, 4 * width), BF),
            pltpu.VMEM((seeds, total, width), BF),
            pltpu.VMEM(flat, F32),
            pltpu.VMEM((count,) + flat, BF),
            pltpu.VMEM((2, seeds, tokens, 2 * token_width), BF),
            pltpu.VMEM(flat, BF),
            pltpu.VMEM((seeds * tokens, token_width), F32),
            pltpu.VMEM(flat, F32),
            pltpu.VMEM((seeds * HEADS, tokens, 128), F32),
            pltpu.VMEM((seeds * HEADS, tokens, 128), F32),
            pltpu.VMEM((HEADS,) + pair_bias.shape[1:], BF),
            pltpu.VMEM(token_project.shape, BF),
            pltpu.VMEM(token_mix.shape, BF),
            pltpu.VMEM(swiglu_in.shape, BF),
            pltpu.VMEM(swiglu_out.shape, BF),
            dma((7,)),
            dma((groups - 1, count // 2)),
            dma((groups - 1, count // 2)),
            dma((hops,)),
            dma((hops,)),
            dma((hops,)),
            dma((hops,)),
            dma((2 * hops + 1,)),
            dma((2 * hops + 1,)),
            dma((4,)),
            dma((4,)),
            dma((4,)),
            dma((4,)),
        ],
        compiler_params=pltpu.CompilerParams(
            vmem_limit_bytes=60 * 1024 * 1024, collective_id=0, has_side_effects=True
        ),
        name="main",
    )(x, enc_bias, index, token_cond, enc_project, enc_mix,
      pool_weight, pair_bias, token_project, token_mix, swiglu_in, swiglu_out, spread_weight,
      dec_bias, dec_project, dec_mix)
    return state.transpose(1, 0, 2), update.transpose(1, 0, 2)


def solution(mesh):
    placed = (
        P("tok", "seed", None),
        P("tok"),
        P("tok", None),
        P("seed", "tok", None),
        P("tok", None, None),
        P("tok", None, None),
    ) + (P(),) * 10
    return jax.shard_map(
        per_device,
        mesh=mesh,
        in_specs=placed,
        out_specs=(P("tok", "seed", None), P("tok", "seed", None)),
        check_vma=False,
    )
```

```python
import functools

import jax
import jax.numpy as jnp
from jax import lax
from jax.experimental import pallas as pl
from jax.experimental.pallas import tpu as pltpu
from jax.sharding import PartitionSpec as P

HEADS = 16
QUERY_BLOCK = 32
EPS = 1e-05
NEGATIVE = -1000000000.0
HALO = 128
RIM = 64
EDGE = 16
MISSING = -1000
BF = jnp.bfloat16
F32 = jnp.float32


def layer_norm(values):
    centre = values - jnp.mean(values, axis=-1, keepdims=True)
    variance = jnp.mean(centre * centre, axis=-1, keepdims=True)
    return centre * lax.rsqrt(variance + EPS)


def mm(a, b):
    return jnp.dot(a, b, preferred_element_type=F32)


def mm_t(a, b):
    return lax.dot_general(a, b, (((1,), (1,)), ((), ())), preferred_element_type=F32)


def iota(shape, dim):
    return lax.broadcasted_iota(jnp.int32, shape, dim)


def window_attention(packed, bias, mixed, first_row, blocks, low, high, group):
    seeds, _, quad = packed.shape
    width = quad // 4
    window = bias.shape[1]
    heads = bias.shape[0] // (QUERY_BLOCK * blocks)
    size = width // heads
    rows = QUERY_BLOCK * heads
    margin = (window - QUERY_BLOCK) // 2
    column = iota((QUERY_BLOCK, width), 1) // size
    lane = iota((rows, window), 1)
    row, source = iota((rows, rows), 0), iota((rows, rows), 1)
    order = (source // heads == row % QUERY_BLOCK) & (source % heads == row // QUERY_BLOCK)
    order = order.astype(BF)

    def step(i, carry):
        scores, places = [], []
        for g in range(group):
            j = i * group + g
            start = pl.multiple_of(first_row - margin + QUERY_BLOCK * j, 16)
            term = mm(order, bias[pl.ds(pl.multiple_of(rows * j, rows), rows), :])
            spot = lane + start
            term = jnp.where((spot >= low) & (spot < high), term, NEGATIVE)
            for s in range(seeds):
                query = packed[s, pl.ds(pl.multiple_of(start + margin, 16), QUERY_BLOCK), :width]
                query = jnp.concatenate(
                    [jnp.where(column == h, query, jnp.zeros_like(query)) for h in range(heads)]
                )
                keys = packed[s, pl.ds(start, window), width : 2 * width]
                scores.append(mm_t(query, keys) * size ** (-0.5) + term)
                places.append((s, j, start))
        weights = [
            jnp.exp(part - jnp.max(part, axis=-1, keepdims=True)).astype(BF) for part in scores
        ]
        sums = [
            mm(part, packed[s, pl.ds(start, window), 2 * width :])
            for part, (s, _, start) in zip(weights, places)
        ]
        for part, (s, j, _) in zip(sums, places):
            part = part[:, :width] / part[:, width:]
            total = part[:QUERY_BLOCK]
            for h in range(1, heads):
                total = jnp.where(column == h, part[QUERY_BLOCK * h : QUERY_BLOCK * (h + 1)], total)
            first = pl.multiple_of(first_row + QUERY_BLOCK * j, QUERY_BLOCK)
            mixed[s, pl.ds(first, QUERY_BLOCK), :] = total.astype(BF)
        return carry

    lax.fori_loop(0, blocks // group, step, 0)


def packed_rows(packed, project, source, begin, end, chunk):
    seeds, _, quad = packed.shape
    used = quad // 4 * 3
    for s in range(seeds):
        for at in range(begin, end, chunk):
            part = layer_norm(source[s, at : at + chunk, :].astype(F32)).astype(BF)
            packed[s, at : at + chunk, :used] = mm(part, project[...]).astype(BF)


def pool_tokens(x, index, cond, mix, pool, enc, residual, mixed):
    seeds, total, width = x.shape
    tokens = cond.shape[0]
    chosen = index == iota((tokens, total), 0)
    counts = jnp.sum(chosen.astype(F32), axis=1, keepdims=True)
    chosen = chosen.astype(BF)
    for s in range(seeds):
        sums = jnp.zeros(residual.shape[1:], F32)
        for at in range(0, total, 256):
            base = x[s, at : at + 256, :].astype(F32)
            part = (base + mm(mixed[s, at : at + 256, :], mix[...])).astype(BF)
            enc[s, at : at + 256, :] = part
            lifted = jnp.maximum(mm(part, pool[...]), 0.0).astype(BF)
            sums = sums + mm(chosen[:, at : at + 256], lifted)
        residual[s] = cond[...].astype(F32) + sums / counts


def head_lanes(size, h, rows):
    first = size * h // 128
    last = (size * h + size - 1) // 128
    spot = iota((rows, (last - first + 1) * 128), 1) + first * 128
    return first, last, (spot >= size * h) & (spot < size * (h + 1))


def attend(first_key, bias, query, kv, attended, tops, sums):
    seeds, tokens, width = query.shape
    keys_here = 2 * tokens
    heads = bias.shape[0]
    size = width // heads
    span = 384
    group = span // size
    where = pl.ds(pl.multiple_of(first_key, keys_here), keys_here)

    def step(i, carry):
        s = i // (heads // group)
        g = i % (heads // group)
        left = pl.multiple_of(g * span, 128)
        tiles = [
            attended[s, :, pl.ds(pl.multiple_of(left + t * 128, 128), 128)]
            for t in range(span // 128)
        ]
        for h in range(group):
            first, last, mine = head_lanes(size, h, tokens)
            wide = (last - first + 1) * 128
            lanes = pl.ds(pl.multiple_of(left + first * 128, 128), wide)
            q = query[s, :, lanes]
            q = jnp.where(mine, q, jnp.zeros_like(q))
            keys = kv[:, s, :, lanes].reshape(keys_here, wide)
            values = kv[:, s, :, pl.ds(pl.multiple_of(left + width + first * 128, 128), wide)]
            scores = mm_t(q, keys) * size ** (-0.5) + bias[g * group + h, :, where].astype(F32)
            spot = s * heads + g * group + h
            before = tops[spot]
            top = jnp.maximum(before, jnp.max(scores, axis=-1, keepdims=True))
            shrink = jnp.exp(before - top)
            weights = jnp.exp(scores - jnp.concatenate([top] * (keys_here // 128), axis=1))
            total = sums[spot] * shrink
            for at in range(0, keys_here, 128):
                total = total + weights[:, at : at + 128]
            tops[spot] = top
            sums[spot] = total
            part = mm(weights.astype(BF), values.reshape(keys_here, wide))
            for t in range(first, last + 1):
                here = slice((t - first) * 128, (t - first + 1) * 128)
                tiles[t] = jnp.where(mine[:, here], tiles[t] * shrink + part[:, here], tiles[t])
        for t, tile in enumerate(tiles):
            attended[s, :, pl.ds(pl.multiple_of(left + t * 128, 128), 128)] = tile
        return carry

    lax.fori_loop(0, seeds * (heads // group), step, 0)


def settle(heads, attended, sums):
    seeds, tokens, width = attended.shape
    size = width // heads
    span = 384
    group = span // size

    def step(i, carry):
        s = i // (heads // group)
        g = i % (heads // group)
        tiles = [jnp.ones((tokens, 128), F32) for _ in range(span // 128)]
        for h in range(group):
            first, last, mine = head_lanes(size, h, tokens)
            total = jnp.sum(sums[s * heads + g * group + h], axis=-1, keepdims=True)
            for t in range(first, last + 1):
                here = slice((t - first) * 128, (t - first + 1) * 128)
                tiles[t] = jnp.where(mine[:, here], total, tiles[t])
        for t, tile in enumerate(tiles):
            lanes = pl.ds(pl.multiple_of(g * span + t * 128, 128), 128)
            attended[s, :, lanes] = attended[s, :, lanes] / tile
        return carry

    lax.fori_loop(0, seeds * (heads // group), step, 0)


def remote(source, target, send, arrive, **place):
    return pltpu.make_async_remote_copy(
        src_ref=source, dst_ref=target, send_sem=send, recv_sem=arrive,
        device_id=place, device_id_type=pl.DeviceIdType.MESH,
    )


def main_kernel(
    count, groups,
    atoms_in, enc_bias_hbm, index_in, cond, enc_project, enc_mix, pool,
    bias_hbm, project_hbm, mix_hbm, wide_hbm, down_hbm, spread_w, dec_bias_hbm, dec_project, dec_mix,
    state_out, out,
    x, atom_bias, low_index, high_index, enc, decoded, spread, dec_bias,
    packed, mixed, residual, everyone, kv, query, gate, attended, tops, sums, bias, project, mix, wide, down,
    sems, bias_send, bias_recv, right_send, right_recv, left_send, left_recv, twin_send, twin_recv,
    up_send, up_recv, down_send, down_recv,
):
    tok = lax.axis_index("tok")
    seed = lax.axis_index("seed")
    chips = count // 2
    inner_tokens = cond.shape[0]
    chip = tok // 2
    twin = tok + 1 - 2 * (tok % 2)
    hops = chips - 1

    barrier = pltpu.get_barrier_semaphore()

    def greet(**place):
        pl.semaphore_signal(
            barrier, inc=1, device_id=place, device_id_type=pl.DeviceIdType.MESH
        )

    greet(tok=twin)
    for k in range(1, groups):
        greet(seed=lax.rem(seed + k, groups))

    @pl.when(chip > 0)
    def _():
        greet(tok=tok - 2)

    @pl.when(chip < chips - 1)
    def _():
        greet(tok=tok + 2)

    side = tok - 1 + 2 * (tok % 2)
    has_side = (side >= 0) & (side < count)

    @pl.when(has_side)
    def _():
        greet(tok=side)

    has_left = jnp.where(chip > 0, 1, 0)
    has_right = jnp.where(chip < chips - 1, 1, 0)
    pl.semaphore_wait(barrier, groups + has_left + has_right + jnp.where(has_side, 1, 0))

    seeds, total, width = x.shape
    inner = total - 2 * HALO
    turn = seeds * HALO
    row, source = iota((turn, turn), 0), iota((turn, turn), 1)
    split = (source == seeds * (row % HALO) + row // HALO).astype(BF)

    def take_in(at):
        part = mm(split, atoms_in[seeds * at : seeds * (at + HALO), :]).astype(BF)
        for s in range(seeds):
            x[s, HALO + at : 2 * HALO + at, :] = part[s * HALO : (s + 1) * HALO]

    take_in(0)
    take_in(inner - HALO)
    heads = enc_bias_hbm.shape[0] // inner
    rim = heads * RIM
    own_bias = heads * inner
    has_below = tok > 0
    has_above = tok < count - 1

    def up(i, source, target):
        return remote(source, target, up_send.at[i], up_recv.at[i], tok=tok + 1)

    def below(i, source, target):
        return remote(source, target, down_send.at[i], down_recv.at[i], tok=tok - 1)

    upward = [
        (0, x.at[:, pl.ds(inner, HALO)], x.at[:, pl.ds(0, HALO)]),
        (1, enc_bias_hbm.at[pl.ds(own_bias - rim, rim)], atom_bias.at[pl.ds(0, rim)]),
        (2, index_in, low_index),
    ]
    downward = [
        (0, x.at[:, pl.ds(HALO, HALO)], x.at[:, pl.ds(HALO + inner, HALO)]),
        (1, enc_bias_hbm.at[pl.ds(0, rim)], atom_bias.at[pl.ds(rim + own_bias, rim)]),
        (2, index_in, high_index),
    ]
    edge_up = (3, spread.at[:, pl.ds(inner_tokens, EDGE)], spread.at[:, pl.ds(0, EDGE)])
    edge_down = (3, spread.at[:, pl.ds(EDGE, EDGE)], spread.at[:, pl.ds(EDGE + inner_tokens, EDGE)])

    @pl.when(has_above)
    def _():
        for part in upward:
            up(*part).start()

    @pl.when(has_below)
    def _():
        for part in downward:
            below(*part).start()

    @pl.when(tok == 0)
    def _():
        x[:, :HALO] = jnp.zeros((seeds, HALO, width), BF)
        atom_bias[:rim] = jnp.zeros((rim, width), BF)
        low_index[...] = jnp.full(low_index.shape, MISSING, jnp.int32)
        spread[:, :EDGE] = jnp.zeros((seeds, EDGE, width), BF)

    @pl.when(tok == count - 1)
    def _():
        x[:, HALO + inner :] = jnp.zeros((seeds, HALO, width), BF)
        atom_bias[rim + own_bias :] = jnp.zeros((rim, width), BF)
        high_index[...] = jnp.full(high_index.shape, MISSING, jnp.int32)
        spread[:, EDGE + inner_tokens :] = jnp.zeros((seeds, EDGE, width), BF)

    share = bias_hbm.shape[0]
    slot = bias.at[pl.ds(seed * share, share)]
    both = jnp.minimum(chip, chips - 1 - chip)

    def offset(p):
        near = (p + 1) // 2
        inside = jnp.where(p % 2 == 1, -near, near)
        outside = jnp.where(chip > chips - 1 - chip, both - p, p - both)
        return jnp.where(p <= 2 * both, inside, outside)

    def event(k):
        return jnp.where(k <= both + 1, max(1, 2 * (k - 1)), both + k)

    def bias_copy(k, p):
        first = pl.multiple_of((chip + offset(p)) * (2 * inner_tokens), 2 * inner_tokens)
        lanes = pl.ds(first, 2 * inner_tokens)
        return remote(
            bias_hbm.at[:, :, lanes], bias.at[pl.ds(seed * share, share), :, lanes],
            bias_send.at[k - 1, p], bias_recv.at[k - 1, p], seed=lax.rem(seed + k, groups),
        )

    square = groups == 4
    beside = seed + 1 - 2 * (seed % 2)
    across = lax.rem(seed + 2, 4)

    def bias_part(i, p, owner, begin, heads_here, target):
        first = pl.multiple_of((chip + offset(p)) * (2 * inner_tokens), 2 * inner_tokens)
        lanes = pl.ds(first, 2 * inner_tokens)
        piece = bias.at[pl.ds(owner * share + begin, heads_here), :, lanes]
        source = bias_hbm.at[:, :, lanes] if i < 2 else piece
        return remote(source, piece, bias_send.at[i, p], bias_recv.at[i, p], seed=target)

    def to_neighbours(p):
        return [bias_part(0, p, seed, 0, share, beside), bias_part(1, p, seed, 0, share, across)]

    def onward(p):
        half = share // 2
        return [
            bias_part(2, p, beside, 0, half, across),
            bias_part(3, p, across, half, share - half, beside),
        ]

    def far_copy():
        first = pl.multiple_of(chip * (2 * inner_tokens), 2 * inner_tokens)
        lanes = pl.ds(first, 2 * inner_tokens)
        return remote(
            bias_hbm.at[:, :, lanes], bias.at[pl.ds(seed * share, share), :, lanes],
            bias_send.at[2, 0], bias_recv.at[2, 0], seed=3 - seed,
        )

    for p in range(chips):
        if square:
            for copy in to_neighbours(p):
                copy.start()
            if p == 0:
                far_copy().start()
        else:
            for k in range(1, groups):
                bias_copy(k, p).start()
    loads = [
        pltpu.make_async_copy(source, target, sems.at[i])
        for i, (source, target) in enumerate(
            (
                (bias_hbm, slot), (project_hbm, project), (mix_hbm, mix), (wide_hbm, wide),
                (down_hbm, down), (dec_bias_hbm, dec_bias),
                (enc_bias_hbm, atom_bias.at[pl.ds(rim, own_bias)]),
            )
        )
    ]
    for load in loads:
        load.start()

    for at in range(HALO, inner - HALO, HALO):
        take_in(at)
    packed[:, :, 3 * width :] = jnp.ones((seeds, total, width), BF)
    mixed[:, :RIM] = jnp.zeros((seeds, RIM, width), BF)
    mixed[:, total - RIM :] = jnp.zeros((seeds, RIM, width), BF)
    packed_rows(packed, enc_project, x, HALO, HALO + inner, 256)

    @pl.when(has_below)
    def _():
        for part in upward:
            up(*part).wait_recv()

    @pl.when(has_above)
    def _():
        for part in downward:
            below(*part).wait_recv()

    packed_rows(packed, enc_project, x, 0, HALO, HALO)
    packed_rows(packed, enc_project, x, HALO + inner, total, HALO)
    low = jnp.where(tok == 0, HALO, 0)
    high = jnp.where(tok == count - 1, HALO + inner, total)
    loads[6].wait()
    blocks = inner // QUERY_BLOCK
    rim_blocks = 2 * RIM // QUERY_BLOCK
    window_attention(packed, atom_bias, mixed, HALO - RIM, blocks + rim_blocks, low, high, 2)
    index = jnp.concatenate(
        [low_index[inner // HALO - 1 :]]
        + [index_in[i : i + 1] for i in range(inner // HALO)]
        + [high_index[:1]],
        axis=1,
    )
    index = index - tok * inner_tokens
    pool_tokens(x, index, cond, enc_mix, pool, enc, residual, mixed)

    tokens, width = cond.shape
    everyone[tok] = layer_norm(residual[...]).astype(BF)

    def to_right(k):
        piece = everyone.at[tok - 2 * k]
        return remote(piece, piece, right_send.at[k], right_recv.at[k], tok=tok + 2)

    def to_left(k):
        piece = everyone.at[tok + 2 * k]
        return remote(piece, piece, left_send.at[k], left_recv.at[k], tok=tok - 2)

    def to_twin(k):
        piece = everyone.at[tok + 2 * k]
        return remote(piece, piece, twin_send.at[hops + k], twin_recv.at[hops + k], tok=twin)

    @pl.when(chip < chips - 1)
    def _():
        to_right(0).start()

    @pl.when(chip > 0)
    def _():
        to_left(0).start()

    to_twin(0).start()

    loads[1].wait()
    own = everyone[tok].reshape(seeds * tokens, width)
    query[...] = mm(own, project[:, :width]).astype(BF).reshape(seeds, tokens, width)
    gate[...] = jax.nn.sigmoid(mm(own, project[:, 3 * width :]))

    attended[...] = jnp.zeros(attended.shape, F32)
    sums[...] = jnp.zeros(sums.shape, F32)
    tops[...] = jnp.full(tops.shape, NEGATIVE, F32)
    loads[0].wait()

    def visit(p, carry):
        for k in range(1, hops + 1):

            @pl.when((p == event(k)) & (chip - k >= 0))
            def _(k=k):
                to_right(k - 1).wait_recv()
                to_twin(-k).start()
                if k < hops:

                    @pl.when(chip < chips - 1)
                    def _():
                        to_right(k).start()

            @pl.when((p == event(k)) & (chip + k < chips))
            def _(k=k):
                to_left(k - 1).wait_recv()
                to_twin(k).start()
                if k < hops:

                    @pl.when(chip > 0)
                    def _():
                        to_left(k).start()

        if square:

            @pl.when(p < chips - 1)
            def _():
                for copy in to_neighbours(p + 1):
                    copy.wait_recv()
                for copy in onward(p + 1):
                    copy.start()

        away = offset(p)
        to_twin(away).wait_recv()
        part = everyone[pl.ds(2 * (chip + away), 2)].reshape(2 * seeds * tokens, width)
        for at in range(0, 2 * width, width):
            piece = mm(part, project[:, width + at : 2 * width + at]).astype(BF)
            kv[:, :, :, at : at + width] = piece.reshape(2, seeds, tokens, width)
        if square:

            @pl.when(p == 0)
            def _():
                for copy in to_neighbours(0) + [far_copy()]:
                    copy.wait_recv()

            @pl.when(p > 0)
            def _():
                for copy in onward(p):
                    copy.wait_recv()
        else:
            for k in range(1, groups):
                bias_copy(k, p).wait_recv()
        attend((chip + away) * (2 * tokens), bias, query, kv, attended, tops, sums)
        return carry

    lax.fori_loop(0, chips, visit, 0)
    settle(bias.shape[0], attended, sums)

    loads[2].wait()
    gated = (attended[...].reshape(seeds * tokens, width) * gate[...]).astype(BF)
    state = residual[...].reshape(seeds * tokens, width) + mm(gated, mix[...])
    part = layer_norm(state).astype(BF)
    loads[3].wait()
    hidden = down.shape[0]
    part = (jax.nn.silu(mm(part, wide[:, :hidden])) * mm(part, wide[:, hidden:])).astype(BF)
    loads[4].wait()
    state = (state + mm(part, down[...])).astype(BF)
    state_out[...] = state.reshape(seeds, tokens, width)
    part = mm(state, spread_w[...]).astype(BF)
    spread[:, EDGE : EDGE + tokens] = part.reshape(seeds, tokens, part.shape[1])

    @pl.when(has_above)
    def _():
        up(*edge_up).start()

    @pl.when(has_below)
    def _():
        below(*edge_down).start()

    @pl.when(has_below)
    def _():
        up(*edge_up).wait_recv()

    @pl.when(has_above)
    def _():
        below(*edge_down).wait_recv()

    picker = (index == iota((tokens + 2 * EDGE, total), 0) - EDGE).astype(BF)
    for s in range(seeds):
        for at in range(0, total, 256):
            carried = lax.dot_general(
                picker[:, at : at + 256], spread[s], (((0,), (0,)), ((), ())),
                preferred_element_type=F32,
            )
            decoded[s, at : at + 256, :] = (
                enc[s, at : at + 256, :].astype(F32) + carried
            ).astype(BF)
    packed_rows(packed, dec_project, decoded, 0, total, 256)
    loads[5].wait()
    window_attention(packed, dec_bias, mixed, HALO, blocks, low, high, 2)
    for s in range(seeds):
        for at in range(HALO, HALO + inner, 256):
            base = decoded[s, at : at + 256, :].astype(F32)
            part = base + mm(mixed[s, at : at + 256, :], dec_mix[...])
            out[s, at - HALO : at - HALO + 256, :] = part.astype(BF)

    @pl.when(has_above)
    def _():
        for part in upward + [edge_up]:
            up(*part).wait_send()

    @pl.when(has_below)
    def _():
        for part in downward + [edge_down]:
            below(*part).wait_send()

    to_twin(0).wait_send()
    for p in range(chips):
        if square:
            for copy in to_neighbours(p) + (onward(p) if p else [far_copy()]):
                copy.wait_send()
        else:
            for k in range(1, groups):
                bias_copy(k, p).wait_send()
    for k in range(hops):

        @pl.when((chip - k >= 0) & (chip < chips - 1))
        def _(k=k):
            to_right(k).wait_send()

        @pl.when((chip + k < chips) & (chip > 0))
        def _(k=k):
            to_left(k).wait_send()

        @pl.when(chip - k - 1 >= 0)
        def _(k=k):
            to_twin(-k - 1).wait_send()

        @pl.when(chip + k + 1 < chips)
        def _(k=k):
            to_twin(k + 1).wait_send()


def per_device(
    atom_feats, atom_index, token_cond, pair_bias, atom_bias_enc, atom_bias_dec,
    enc_project, enc_mix, pool_weight, token_project, token_mix, swiglu_in, swiglu_out,
    spread_weight, dec_project, dec_mix,
):
    atoms, seeds, width = atom_feats.shape
    tokens, token_width = token_cond.shape
    atom_heads, window = atom_bias_enc.shape[1:]
    count = lax.axis_size("tok")
    x = atom_feats.reshape(atoms * seeds, width)

    enc_bias = atom_bias_enc.reshape(atoms * atom_heads, window)
    dec_bias = atom_bias_dec.reshape(atoms * atom_heads, window)
    index = atom_index.reshape(atoms // HALO, HALO)
    total = atoms + 2 * HALO
    groups = lax.axis_size("seed")
    hops = max(count // 2 - 1, 1)
    vmem = pl.BlockSpec(memory_space=pltpu.VMEM)
    hbm = pl.BlockSpec(memory_space=pl.ANY)
    flat = (seeds, tokens, token_width)
    dma = pltpu.SemaphoreType.DMA
    state, update = pl.pallas_call(
        functools.partial(main_kernel, count, groups),
        out_shape=(
            jax.ShapeDtypeStruct(flat, BF),
            jax.ShapeDtypeStruct((seeds, atoms, width), BF),
        ),
        in_specs=[vmem, hbm] + [vmem] * 5 + [hbm] * 5 + [vmem, hbm, vmem, vmem],
        scratch_shapes=[
            pltpu.VMEM((seeds, total, width), BF),
            pltpu.VMEM(((atoms + 2 * RIM) * atom_heads, window), BF),
            pltpu.VMEM(index.shape, jnp.int32),
            pltpu.VMEM(index.shape, jnp.int32),
            pltpu.VMEM((seeds, total, width), BF),
            pltpu.VMEM((seeds, total, width), BF),
            pltpu.VMEM((seeds, tokens + 2 * EDGE, width), BF),
            pltpu.VMEM(dec_bias.shape, BF),
            pltpu.VMEM((seeds, total, 4 * width), BF),
            pltpu.VMEM((seeds, total, width), BF),
            pltpu.VMEM(flat, F32),
            pltpu.VMEM((count,) + flat, BF),
            pltpu.VMEM((2, seeds, tokens, 2 * token_width), BF),
            pltpu.VMEM(flat, BF),
            pltpu.VMEM((seeds * tokens, token_width), F32),
            pltpu.VMEM(flat, F32),
            pltpu.VMEM((seeds * HEADS, tokens, 128), F32),
            pltpu.VMEM((seeds * HEADS, tokens, 128), F32),
            pltpu.VMEM((HEADS,) + pair_bias.shape[1:], BF),
            pltpu.VMEM(token_project.shape, BF),
            pltpu.VMEM(token_mix.shape, BF),
            pltpu.VMEM(swiglu_in.shape, BF),
            pltpu.VMEM(swiglu_out.shape, BF),
            dma((7,)),
            dma((groups, count // 2)),
            dma((groups, count // 2)),
            dma((hops,)),
            dma((hops,)),
            dma((hops,)),
            dma((hops,)),
            dma((2 * hops + 1,)),
            dma((2 * hops + 1,)),
            dma((4,)),
            dma((4,)),
            dma((4,)),
            dma((4,)),
        ],
        compiler_params=pltpu.CompilerParams(
            vmem_limit_bytes=50 * 1024 * 1024, collective_id=0, has_side_effects=True
        ),
        name="main",
    )(x, enc_bias, index, token_cond, enc_project, enc_mix,
      pool_weight, pair_bias, token_project, token_mix, swiglu_in, swiglu_out, spread_weight,
      dec_bias, dec_project, dec_mix)
    return state.transpose(1, 0, 2), update.transpose(1, 0, 2)


def solution(mesh):
    placed = (
        P("tok", "seed", None),
        P("tok"),
        P("tok", None),
        P("seed", "tok", None),
        P("tok", None, None),
        P("tok", None, None),
    ) + (P(),) * 10
    return jax.shard_map(
        per_device,
        mesh=mesh,
        in_specs=placed,
        out_specs=(P("tok", "seed", None), P("tok", "seed", None)),
        check_vma=False,
    )
```
